256 devices in a mesh: samp: 32 (over x, z), tp: 8 (over y, core).
Axes of the slice: x: 4, y: 4, z: 8, core: 2. Of those that a mesh axis runs over, the one named last changes fastest.
Arguments:
- append_states: bfloat16 [8192, 5120], P('samp'), may hold values from -6 to 6
- kv_weight: bfloat16 [5120, 2, 1024], P(None, None, 'tp'), may hold values from -0.078125 to 0.078125
- key_gain: float32 [128], replicated, may hold values from 0.1 to 1.9
- queries: bfloat16 [128, 4096], P('samp', 'tp'), may hold values from -128 to 128
- res_keys: bfloat16 [512, 128, 1024], P('samp', None, 'tp'), may hold values from -6 to 6
- res_values: bfloat16 [512, 128, 1024], P('samp', None, 'tp'), may hold values from -6 to 6
- page_table: int32 [128, 4], P('samp'), may hold values from 0 to 15, as said below
- diverge: int32 [128], replicated, may hold values from 1 to 4, as said below
- lengths: int32 [128], replicated, may hold values from 129 to 8704, as said below
- out_weight: bfloat16 [4096, 5120], P('tp'), may hold values from -0.5 to 0.5
Outputs:
- mixed: bfloat16 [128, 5120], P('samp')
The draws below stay inside these ranges and needn't reach their ends.
Inputs may be any that keep to these rules, and one draw needn't show every extreme that they name: `page_table`: the rows of samples 4 * d to 4 * d + 3 together name every slot 0 to 15 exactly once. `diverge`: some sample has 4 and some has 1. lengths[s] - 128 * diverge[s] lies in 1 to 8192; it is 8192 for some sample with diverge 4, and 1 for some sample with diverge 1.
All inputs are finite; a program needn't handle non-finite values.
Results may differ from the reference program's by a relative error of at most 0.018.
The reference program's roundings to bfloat16 on the way (of `app_keys`, `app_values`, `rounded_weights` and `attended`) count: a program that leaves them out, or rounds other values in their place, can miss the bound.
Values may be sent and summed in bfloat16 or wider, within the bound.
A program may use at most 64 MiB of HBM per device.

```python
import jax
import jax.numpy as jnp
from jax import lax

D = 5120
H = 32
KVH = 8
HD = 128
PAGE = 128
RES = 4
SAMP_DEV = 4
SAMPLES = 128
APPEND = 8192
SLOTS = 16
POOL = 512
N_SAMP = 32


def shared_counts(key):
    order = jax.random.permutation(jax.random.fold_in(key, 101), SAMPLES)
    pages = jax.random.randint(jax.random.fold_in(key, 102), (SAMPLES,), 1, RES + 1)
    extra = jax.random.randint(jax.random.fold_in(key, 103), (SAMPLES,), 1, APPEND + 1)
    pages = pages.at[order[0]].set(RES).at[order[1]].set(1)
    extra = extra.at[order[0]].set(APPEND).at[order[1]].set(1)
    return (pages.astype(jnp.int32), extra.astype(jnp.int32))


def draw_diverge(key, part):
    pages, extra = shared_counts(key)
    return pages


def draw_lengths(key, part):
    pages, extra = shared_counts(key)
    return (pages * PAGE + extra).astype(jnp.int32)


def draw_page_table(key, part):
    key = jax.random.fold_in(key, 7)
    device_keys = jax.random.split(key, N_SAMP)
    tables = jax.vmap(lambda device_key: jax.random.permutation(device_key, SLOTS))(device_keys)
    return tables.reshape(SAMPLES, RES).astype(jnp.int32)


def draw_queries(key, part):
    key = jax.random.fold_in(key, 9)
    values = jnp.clip(2.0 * jax.random.normal(jax.random.fold_in(key, 3), (SAMPLES, H * HD), jnp.float32), -12.0, 12.0)
    return values.astype(jnp.bfloat16)


def shard_levels(stream_key, extent, pieces, least, top_value):
    def one(dim, parts):
        steps = jax.random.uniform(jax.random.fold_in(jax.random.fold_in(stream_key, 6), dim), (parts,), jnp.float32, least / len(pieces), top_value / len(pieces))
        return jnp.repeat(jnp.exp(steps), extent[dim] // parts).reshape((-1,) + (1,) * (len(extent) - dim - 1))

    level = one(*pieces[0])
    for cut in pieces[1:]:
        level = level * one(*cut)
    return level


def noise(key, extent, scale, limit, cuts=(), kind=jnp.bfloat16):
    loudness = shard_levels(key, extent, cuts, -0.22, 0.18) if cuts else 1.0
    values = jax.random.normal(key, extent, jnp.float32) * scale * loudness
    return jnp.minimum(jnp.maximum(values, -limit), limit).astype(kind)


def setup_inputs(seed: int = 0) -> dict:
    streams_of = jax.random.split(jax.random.key(seed), 11)
    return {
        "append_states": noise(streams_of[0], (APPEND, D), 1.0, 6.0, ((0, 32),)),
        "kv_weight": noise(streams_of[1], (D, 2, KVH * HD), D ** -0.5, 0.078125, ((2, 8),)),
        "key_gain": jnp.clip(1.0 + 0.18 * jax.random.normal(streams_of[2], (HD,), jnp.float32), 0.1, 1.9),
        "queries": draw_queries(jax.random.fold_in(streams_of[10], 71), 0),
        "res_keys": noise(streams_of[4], (POOL, PAGE, KVH * HD), 1.0, 6.0, ((0, 32), (2, 8))),
        "res_values": noise(streams_of[5], (POOL, PAGE, KVH * HD), 1.0, 6.0, ((0, 32), (2, 8))),
        "page_table": draw_page_table(jax.random.fold_in(streams_of[10], 71), 0),
        "diverge": draw_diverge(jax.random.fold_in(streams_of[10], 71), 0),
        "lengths": draw_lengths(jax.random.fold_in(streams_of[10], 71), 0),
        "out_weight": noise(streams_of[9], (H * HD, D), HD ** -0.5, 0.5, ((0, 8),)),
    }


ROPE_BASE = 1000000.0
NORM_EPS = 1e-06
FLOOR = -1e+30

def rotate(vectors, positions):
    half_width = vectors.shape[-1] // 2
    frequency = ROPE_BASE ** (-(jnp.arange(half_width, dtype=jnp.float32) * 2.0 / vectors.shape[-1]))
    angles = positions.astype(jnp.float32)[..., None] * frequency
    cosine = jnp.cos(angles)
    sine_part = jnp.sin(angles)
    first_part = vectors[..., :half_width]
    second_part = vectors[..., half_width:]
    return jnp.concatenate([first_part * cosine - second_part * sine_part, second_part * cosine + first_part * sine_part], axis=-1)

def reference(append_states, kv_weight, key_gain, queries, res_keys, res_values, page_table, diverge, lengths, out_weight):
    group_size = H // KVH
    projected = jnp.dot(append_states, kv_weight.reshape(D, 2 * KVH * HD), preferred_element_type=jnp.float32).reshape(APPEND, 2, KVH, HD)
    raw_keys = projected[:, 0]
    key_scale = lax.rsqrt(lax.optimization_barrier(jnp.mean(raw_keys * raw_keys, axis=-1, keepdims=True)) + NORM_EPS)
    app_positions = jnp.arange(APPEND, dtype=jnp.int32)
    app_keys = rotate(raw_keys * key_scale * key_gain, app_positions[:, None]).astype(jnp.bfloat16)
    app_values = projected[:, 1].astype(jnp.bfloat16)
    context_rows = RES * PAGE

    def one_sample(sample):
        slot_rows = page_table[sample] + sample // SAMP_DEV * SLOTS
        own_keys = res_keys[slot_rows].reshape(context_rows, KVH, HD)
        own_values = res_values[slot_rows].reshape(context_rows, KVH, HD)
        div_here = diverge[sample]
        len_here = lengths[sample]
        query_row = queries[sample].astype(jnp.float32).reshape(H, HD)
        query_res = rotate(query_row, len_here).astype(jnp.bfloat16).reshape(KVH, group_size, HD)
        query_app = rotate(query_row, len_here - PAGE * div_here).astype(jnp.bfloat16).reshape(KVH, group_size, HD)
        score_res = jnp.einsum('kgd,tkd->kgt', query_res.astype(jnp.float32), own_keys.astype(jnp.float32))
        score_app = jnp.einsum('kgd,tkd->kgt', query_app.astype(jnp.float32), app_keys.astype(jnp.float32))
        scores = jnp.concatenate([score_res, score_app], axis=-1) * HD ** (-0.5)
        valid_keys = jnp.concatenate([jnp.arange(context_rows, dtype=jnp.int32) < PAGE * div_here, jnp.arange(APPEND, dtype=jnp.int32) < len_here - PAGE * div_here])
        highest = lax.optimization_barrier(jnp.max(jnp.where(valid_keys, scores, FLOOR), axis=-1, keepdims=True))
        weights = jnp.where(valid_keys, jnp.exp(scores - highest), 0.0)
        totals = lax.optimization_barrier(jnp.sum(weights, axis=-1))
        rounded_weights = lax.optimization_barrier(weights.astype(jnp.bfloat16)).astype(jnp.float32)
        all_values = jnp.concatenate([own_values, app_values], axis=0).astype(jnp.float32)
        attended = jnp.einsum('kgt,tkd->kgd', rounded_weights, all_values) / totals[..., None]
        return attended.reshape(H * HD).astype(jnp.bfloat16)
    attended = lax.map(one_sample, jnp.arange(SAMPLES, dtype=jnp.int32))
    return jnp.dot(attended, out_weight, preferred_element_type=jnp.float32).astype(jnp.bfloat16)
```

```python
import numpy as np
import jax
import jax.numpy as jnp
from jax import lax
from jax.experimental import pallas as pl
from jax.experimental.pallas import tpu as pltpu
from jax.sharding import PartitionSpec as P

ROPE_BASE = 1000000.0
NORM_EPS = 1e-06
FLOOR = -1e30
S = 32
T = 8
HD = 128
D = 5120
ROWS = 256
NC = 5
DC = D // NC
COLS = D // T
MESH = pl.DeviceIdType.MESH

COS0, SIN0, COSB, SINB, FREQ = 0, 256, 512, 544, 576


def rope_table():
    freq = ROPE_BASE ** (-(np.arange(64, dtype=np.float64) * 2.0 / HD))
    freq = np.concatenate([freq, freq])
    row = np.arange(ROWS, dtype=np.float64)[:, None] * freq
    base = (np.arange(S, dtype=np.float64) * ROWS)[:, None] * freq
    last = np.zeros((8, HD))
    last[:] = freq
    return np.concatenate([np.cos(row), np.sin(row), np.cos(base), np.sin(base), last]).astype(
        np.float32
    )


def swap_halves(v):
    lane = lax.broadcasted_iota(jnp.int32, v.shape, 1)
    return jnp.where(lane < 64, -1.0, 1.0) * pltpu.roll(v, 64, 1)


def kernel(
    x_hbm,
    w_hbm,
    gain_hbm,
    q_hbm,
    rk_hbm,
    rv_hbm,
    pt_hbm,
    div_hbm,
    len_hbm,
    ow_hbm,
    tab_hbm,
    out_ref,
    x_v,
    w_v,
    wd,
    gain_v,
    q_v,
    rk_v,
    rv_v,
    pt_s,
    div_s,
    len_s,
    div_v,
    len_v,
    ow_v,
    tab_v,
    q_send,
    q_res,
    q_all,
    o_send,
    o_all,
    st_send,
    st_all,
    tr_v,
    rs_send,
    rs_all,
    ag,
    small_sem,
    chunk_sem,
    page_sem,
    ow_sem,
    send_sem,
    recv_sem,
):
    me = lax.axis_index("samp")
    mt = lax.axis_index("tp")

    small = [
        pltpu.make_async_copy(src, dst, small_sem.at[i])
        for i, (src, dst) in enumerate(
            [
                (len_hbm, len_s),
                (div_hbm, div_s),
                (q_hbm, q_v),
                (tab_hbm, tab_v),
                (pt_hbm, pt_s),
                (len_hbm, len_v),
                (div_hbm, div_v),
                (gain_hbm, gain_v),
            ]
        )
    ]
    for copy in small:
        copy.start()
    w_copies = [
        pltpu.make_async_copy(
            w_hbm.at[pl.ds(c * 2 * DC, 2 * DC)], w_v.at[pl.ds(c * 2 * DC, 2 * DC)], chunk_sem.at[0, c]
        )
        for c in range(NC)
    ]
    x_copies = [
        pltpu.make_async_copy(
            x_hbm.at[:, pl.ds(c * DC, DC)], x_v.at[:, pl.ds(c * DC, DC)], chunk_sem.at[1, c]
        )
        for c in range(NC)
    ]
    for c in range(NC):
        w_copies[c].start()
        x_copies[c].start()
    pages = [
        pltpu.make_async_copy(rk_hbm, rk_v, page_sem.at[0]),
        pltpu.make_async_copy(rv_hbm, rv_v, page_sem.at[1]),
    ]
    for copy in pages:
        copy.start()
    ow_copy = pltpu.make_async_copy(ow_hbm, ow_v, ow_sem)
    ow_copy.start()

    barrier = pltpu.get_barrier_semaphore()

    @pl.loop(1, S)
    def _(k):
        pl.semaphore_signal(
            barrier, inc=1, device_id={"samp": lax.rem(me + k, S)}, device_id_type=MESH
        )

    @pl.loop(1, T)
    def _(k):
        pl.semaphore_signal(
            barrier, inc=1, device_id={"tp": lax.rem(mt + k, T)}, device_id_type=MESH
        )

    for copy in small:
        copy.wait()
    row = lax.broadcasted_iota(jnp.int32, (16, HD), 0)
    sample = lax.rem(row, 4)

    def by_sample(values):
        return jnp.where(
            sample == 0,
            values[0],
            jnp.where(sample == 1, values[1], jnp.where(sample == 2, values[2], values[3])),
        )

    my_len = [len_s[0, me * 4 + i] for i in range(4)]
    my_div = [div_s[0, me * 4 + i] for i in range(4)]
    freq = tab_v[FREQ : FREQ + 1, :]
    q = q_v[...].astype(jnp.float32)
    q = jnp.concatenate([q[:, h * HD : (h + 1) * HD] for h in range(4)], axis=0)
    q_swapped = swap_halves(q)

    def rotate(positions):
        angle = by_sample(positions).astype(jnp.float32) * freq
        return (q * jnp.cos(angle) + q_swapped * jnp.sin(angle)).astype(jnp.bfloat16)

    q_app = rotate([my_len[i] - 128 * my_div[i] for i in range(4)])
    q_res[...] = rotate(my_len)
    q_send[...] = q_app
    q_all[me] = q_app

    pl.semaphore_wait(barrier, S - 1 + T - 1)

    @pl.loop(1, S)
    def _(k):
        pltpu.make_async_remote_copy(
            src_ref=q_send,
            dst_ref=q_all.at[me],
            send_sem=send_sem.at[0],
            recv_sem=recv_sem.at[0],
            device_id={"samp": lax.rem(me + k, S)},
            device_id_type=MESH,
        ).start()

    used = len_v[...] - 128 * div_v[...]
    high = lax.shift_right_logical(used, 7)
    low = used - 128 * high
    pair_row = lax.broadcasted_iota(jnp.int32, (16, 128), 0)
    pair = jnp.where(pair_row == 0, high, jnp.where(pair_row == 1, low, 0))
    e_row = lax.broadcasted_iota(jnp.int32, (128, 512), 0)
    e_col = lax.broadcasted_iota(jnp.int32, (128, 512), 1)
    spread = jnp.where(
        e_row == 4 * lax.shift_right_logical(e_col, 4) + jnp.bitwise_and(e_col, 3), 1.0, 0.0
    ).astype(jnp.bfloat16)
    wide = jnp.dot(
        pair.astype(jnp.float32).astype(jnp.bfloat16), spread, preferred_element_type=jnp.float32
    )
    used_wide = (wide[0:1] * 128.0 + wide[1:2]).astype(jnp.int32)

    p_row = lax.broadcasted_iota(jnp.int32, (256, 256), 0)
    p_col = lax.broadcasted_iota(jnp.int32, (256, 256), 1)
    perm = jnp.where(
        p_col == jnp.where(p_row < 128, 2 * p_row, 2 * p_row - 255), 1.0, 0.0
    ).astype(jnp.bfloat16)
    acc = jnp.zeros((ROWS, 256), jnp.float32)
    for c in range(NC):
        w_copies[c].wait()
        for i in range(c * DC // 256, (c + 1) * DC // 256):
            pairs = jnp.concatenate(
                [w_v[pl.ds(i * 512, 256), :], w_v[pl.ds(i * 512 + 256, 256), :]], axis=1
            )
            apart = jnp.dot(perm, pairs, preferred_element_type=jnp.float32).astype(jnp.bfloat16)
            wd[pl.ds(i * 256, 128), 0:128] = apart[0:128, 0:128]
            wd[pl.ds(i * 256, 128), 128:256] = apart[128:256, 0:128]
            wd[pl.ds(i * 256 + 128, 128), 0:128] = apart[0:128, 128:256]
            wd[pl.ds(i * 256 + 128, 128), 128:256] = apart[128:256, 128:256]
        x_copies[c].wait()
        acc = acc + jnp.dot(
            x_v[:, c * DC : (c + 1) * DC],
            wd[c * DC : (c + 1) * DC, :],
            preferred_element_type=jnp.float32,
        )
    raw = acc[:, 0:128]
    values = acc[:, 128:256].astype(jnp.bfloat16)
    scale = lax.rsqrt(jnp.mean(raw * raw, axis=1, keepdims=True) + NORM_EPS)
    keys = raw * scale * gain_v[...]
    cos_b = tab_v[pl.ds(COSB + me, 1), :]
    sin_b = tab_v[pl.ds(SINB + me, 1), :]
    cos_0 = tab_v[COS0 : COS0 + ROWS, :]
    sin_0 = tab_v[SIN0 : SIN0 + ROWS, :]
    cos = cos_0 * cos_b - sin_0 * sin_b
    sin = sin_0 * cos_b + cos_0 * sin_b
    keys = (keys * cos + swap_halves(keys) * sin).astype(jnp.bfloat16)

    pltpu.make_async_copy(
        q_all.at[pl.ds(0, S - 1)], q_all.at[pl.ds(0, S - 1)], recv_sem.at[0]
    ).wait()
    scores = lax.dot_general(
        keys,
        q_all[...].reshape(S * 16, HD),
        (((1,), (1,)), ((), ())),
        preferred_element_type=jnp.float32,
    ) * (HD**-0.5)
    position = lax.broadcasted_iota(jnp.int32, (ROWS, S * 16), 0) + me * ROWS
    valid = position < used_wide
    top = jnp.max(jnp.where(valid, scores, FLOOR), axis=0, keepdims=True)
    weights = jnp.where(valid, jnp.exp(scores - top), 0.0)
    total = jnp.sum(weights, axis=0, keepdims=True)
    part = lax.dot_general(
        weights.astype(jnp.bfloat16),
        values,
        (((0,), (0,)), ((), ())),
        preferred_element_type=jnp.float32,
    )
    o_send[...] = part.astype(jnp.bfloat16).reshape(S, 16, HD)
    for g in range(4):
        st_send[g, 0:1, :] = top[:, g * 128 : (g + 1) * 128]
        st_send[g, 1:2, :] = total[:, g * 128 : (g + 1) * 128]

    @pl.loop(1, S)
    def _(k):
        peer = lax.rem(me + k, S)
        pltpu.make_async_remote_copy(
            src_ref=o_send.at[peer],
            dst_ref=o_all.at[me],
            send_sem=send_sem.at[1],
            recv_sem=recv_sem.at[1],
            device_id={"samp": peer},
            device_id_type=MESH,
        ).start()
        pltpu.make_async_remote_copy(
            src_ref=st_send.at[peer // 8],
            dst_ref=st_all.at[me],
            send_sem=send_sem.at[2],
            recv_sem=recv_sem.at[2],
            device_id={"samp": peer},
            device_id_type=MESH,
        ).start()

    o_all[me] = o_send[me]
    st_all[me] = st_send[me // 8]

    for copy in pages:
        copy.wait()
    lane = lax.broadcasted_iota(jnp.int32, (16, HD), 1)
    slot_ok = jnp.zeros((16, HD), jnp.float32)
    for j in range(4):
        page = by_sample([pt_s[i, j] for i in range(4)])
        count = by_sample(my_div)
        slot_ok = jnp.where((lane == page) & (count > j), 1.0, slot_ok)
    seen = jnp.concatenate(
        [jnp.broadcast_to(slot_ok[:, k : k + 1], (16, HD)) for k in range(16)], axis=1
    ) > 0.5
    res_scores = lax.dot_general(
        q_res[...], rk_v[...], (((1,), (1,)), ((), ())), preferred_element_type=jnp.float32
    ) * (HD**-0.5)
    res_top = jnp.max(jnp.where(seen, res_scores, FLOOR), axis=1, keepdims=True)
    res_weights = jnp.where(seen, jnp.exp(res_scores - res_top), 0.0)
    res_total = jnp.sum(res_weights, axis=1, keepdims=True)
    res_part = jnp.dot(
        res_weights.astype(jnp.bfloat16), rv_v[...], preferred_element_type=jnp.float32
    )

    pltpu.make_async_copy(
        st_all.at[pl.ds(0, S - 1)], st_all.at[pl.ds(0, S - 1)], recv_sem.at[2]
    ).wait()
    pltpu.make_async_copy(
        o_all.at[pl.ds(0, S - 1)], o_all.at[pl.ds(0, S - 1)], recv_sem.at[1]
    ).wait()
    tops = jnp.concatenate([st_all[:, 0, :], jnp.full((128 - S, 128), FLOOR, jnp.float32)], axis=0)
    totals = jnp.concatenate([st_all[:, 1, :], jnp.zeros((128 - S, 128), jnp.float32)], axis=0)
    tr_v[0] = tops.T
    tr_v[1] = totals.T
    mine = pl.multiple_of(16 * lax.rem(me, 8), 16)
    tops = tr_v[0, pl.ds(mine, 16), :]
    totals = tr_v[1, pl.ds(mine, 16), :]
    highest = jnp.maximum(jnp.max(tops, axis=1, keepdims=True), res_top)
    factor = jnp.exp(tops - highest)
    res_factor = jnp.exp(res_top - highest)
    whole = jnp.sum(factor * totals, axis=1, keepdims=True) + res_factor * res_total
    attended = res_part * res_factor
    for i in range(S):
        attended = attended + factor[:, i : i + 1] * o_all[i].astype(jnp.float32)
    attended = attended / whole
    attended = jnp.concatenate(
        [attended if h == 0 else pltpu.roll(attended, 16 - 4 * h, 0) for h in range(4)], axis=1
    ).astype(jnp.bfloat16)

    ow_copy.wait()

    @pl.loop(1, T)
    def _(k):
        peer = lax.rem(mt + k, T)
        columns = pl.ds(pl.multiple_of(peer * COLS, COLS), COLS)
        piece = jnp.dot(attended, ow_v[:, columns], preferred_element_type=jnp.float32)
        rs_send[peer] = piece[0:4, :]
        pltpu.make_async_remote_copy(
            src_ref=rs_send.at[peer],
            dst_ref=rs_all.at[mt],
            send_sem=send_sem.at[3],
            recv_sem=recv_sem.at[3],
            device_id={"tp": peer},
            device_id_type=MESH,
        ).start()

    columns = pl.ds(pl.multiple_of(mt * COLS, COLS), COLS)
    rs_all[mt] = jnp.dot(attended, ow_v[:, columns], preferred_element_type=jnp.float32)[0:4, :]
    pltpu.make_async_copy(
        rs_all.at[pl.ds(0, T - 1)], rs_all.at[pl.ds(0, T - 1)], recv_sem.at[3]
    ).wait()
    piece = rs_all[0]
    for t in range(1, T):
        piece = piece + rs_all[t]
    ag[mt] = piece

    @pl.loop(1, T)
    def _(k):
        pltpu.make_async_remote_copy(
            src_ref=ag.at[mt],
            dst_ref=ag.at[mt],
            send_sem=send_sem.at[4],
            recv_sem=recv_sem.at[4],
            device_id={"tp": lax.rem(mt + k, T)},
            device_id_type=MESH,
        ).start()

    pltpu.make_async_copy(
        ag.at[pl.ds(0, T - 1)], ag.at[pl.ds(0, T - 1)], recv_sem.at[4]
    ).wait()
    for t in range(T):
        out_ref[:, t * COLS : (t + 1) * COLS] = ag[t].astype(jnp.bfloat16)

    for sem, buffer, n in ((0, q_all, S), (1, o_all, S), (2, st_all, S), (3, rs_all, T), (4, ag, T)):
        part_ref = buffer.at[pl.ds(0, n - 1)]
        pltpu.make_async_copy(part_ref, part_ref, send_sem.at[sem]).wait()


def local(x, w, gain, q, rk, rv, pt, div, length, ow):
    bf16, f32, i32 = jnp.bfloat16, jnp.float32, jnp.int32
    hbm = pl.BlockSpec(memory_space=pl.ANY)
    V = pltpu.VMEM
    return pl.pallas_call(
        kernel,
        out_shape=jax.ShapeDtypeStruct((4, D), bf16),
        in_specs=[hbm] * 11,
        out_specs=pl.BlockSpec(memory_space=pltpu.VMEM),
        scratch_shapes=[
            V((ROWS, D), bf16),
            V((2 * D, HD), bf16),
            V((D, 256), bf16),
            V((1, HD), f32),
            V((4, 512), bf16),
            V((2048, HD), bf16),
            V((2048, HD), bf16),
            pltpu.SMEM((4, 4), i32),
            pltpu.SMEM((1, 128), i32),
            pltpu.SMEM((1, 128), i32),
            V((1, 128), i32),
            V((1, 128), i32),
            V((512, D), bf16),
            V((584, HD), f32),
            V((16, HD), bf16),
            V((16, HD), bf16),
            V((S, 16, HD), bf16),
            V((S, 16, HD), bf16),
            V((S, 16, HD), bf16),
            V((4, 2, 128), f32),
            V((S, 2, 128), f32),
            V((2, 128, 128), f32),
            V((T, 4, COLS), f32),
            V((T, 4, COLS), f32),
            V((T, 4, COLS), f32),
            pltpu.SemaphoreType.DMA((8,)),
            pltpu.SemaphoreType.DMA((2, NC)),
            pltpu.SemaphoreType.DMA((2,)),
            pltpu.SemaphoreType.DMA,
            pltpu.SemaphoreType.DMA((5,)),
            pltpu.SemaphoreType.DMA((5,)),
        ],
        compiler_params=pltpu.CompilerParams(
            collective_id=0, has_side_effects=True, vmem_limit_bytes=40 * 1024 * 1024
        ),
        cost_estimate=pl.CostEstimate(
            flops=1_500_000_000, bytes_accessed=12_000_000, transcendentals=200_000
        ),
    )(
        x,
        w.reshape(2 * D, HD),
        gain.reshape(1, HD),
        q,
        rk.reshape(2048, HD),
        rv.reshape(2048, HD),
        pt,
        div.reshape(1, 128),
        length.reshape(1, 128),
        ow,
        jnp.asarray(rope_table()),
    )


def solution(mesh):
    return jax.shard_map(
        local,
        mesh=mesh,
        in_specs=(
            P("samp", None),
            P(None, None, "tp"),
            P(),
            P("samp", "tp"),
            P("samp", None, "tp"),
            P("samp", None, "tp"),
            P("samp", None),
            P(),
            P(),
            P("tp", None),
        ),
        out_specs=P("samp", None),
        check_vma=False,
    )
```

```python
import numpy as np
import jax
import jax.numpy as jnp
from jax import lax
from jax.experimental import pallas as pl
from jax.experimental.pallas import tpu as pltpu
from jax.sharding import PartitionSpec as P

ROPE_BASE = 1000000.0
NORM_EPS = 1e-06
FLOOR = -1e30
S = 32
T = 8
HD = 128
D = 5120
ROWS = 256
NC = 5
DC = D // NC
COLS = D // T
MESH = pl.DeviceIdType.MESH

COS0, SIN0, COSB, SINB, FREQ = 0, 256, 512, 544, 576


def rope_table():
    freq = ROPE_BASE ** (-(np.arange(64, dtype=np.float64) * 2.0 / HD))
    freq = np.concatenate([freq, freq])
    row = np.arange(ROWS, dtype=np.float64)[:, None] * freq
    base = (np.arange(S, dtype=np.float64) * ROWS)[:, None] * freq
    last = np.zeros((8, HD))
    last[:] = freq
    return np.concatenate([np.cos(row), np.sin(row), np.cos(base), np.sin(base), last]).astype(
        np.float32
    )


def swap_halves(v):
    lane = lax.broadcasted_iota(jnp.int32, v.shape, 1)
    return jnp.where(lane < 64, -1.0, 1.0) * pltpu.roll(v, 64, 1)


def kernel(
    x_hbm,
    w_hbm,
    gain_hbm,
    q_hbm,
    rk_hbm,
    rv_hbm,
    pt_hbm,
    div_hbm,
    len_hbm,
    ow_hbm,
    tab_hbm,
    out_ref,
    x_v,
    w_v,
    wd,
    gain_v,
    q_v,
    rk_v,
    rv_v,
    pt_s,
    div_s,
    len_s,
    div_v,
    len_v,
    ow_v,
    tab_v,
    q_send,
    q_res,
    q_all,
    o_send,
    o_all,
    st_send,
    st_all,
    tr_v,
    rs_send,
    rs_all,
    ag,
    small_sem,
    chunk_sem,
    page_sem,
    ow_sem,
    send_sem,
    recv_sem,
):
    me = lax.axis_index("samp")
    mt = lax.axis_index("tp")

    small = [
        pltpu.make_async_copy(src, dst, small_sem.at[i])
        for i, (src, dst) in enumerate(
            [
                (len_hbm, len_s),
                (div_hbm, div_s),
                (q_hbm, q_v),
                (tab_hbm, tab_v),
                (pt_hbm, pt_s),
                (len_hbm, len_v),
                (div_hbm, div_v),
                (gain_hbm, gain_v),
            ]
        )
    ]
    for copy in small:
        copy.start()
    w_copies = [
        pltpu.make_async_copy(
            w_hbm.at[pl.ds(c * 2 * DC, 2 * DC)], w_v.at[pl.ds(c * 2 * DC, 2 * DC)], chunk_sem.at[0, c]
        )
        for c in range(NC)
    ]
    x_copies = [
        pltpu.make_async_copy(
            x_hbm.at[:, pl.ds(c * DC, DC)], x_v.at[:, pl.ds(c * DC, DC)], chunk_sem.at[1, c]
        )
        for c in range(NC)
    ]
    for c in range(NC):
        w_copies[c].start()
        x_copies[c].start()
    pages = [
        pltpu.make_async_copy(rk_hbm, rk_v, page_sem.at[0]),
        pltpu.make_async_copy(rv_hbm, rv_v, page_sem.at[1]),
    ]
    for copy in pages:
        copy.start()
    ow_copy = pltpu.make_async_copy(ow_hbm, ow_v, ow_sem)
    ow_copy.start()

    barrier = pltpu.get_barrier_semaphore()

    @pl.loop(1, S)
    def _(k):
        pl.semaphore_signal(
            barrier, inc=1, device_id={"samp": lax.rem(me + k, S)}, device_id_type=MESH
        )

    @pl.loop(1, T)
    def _(k):
        pl.semaphore_signal(
            barrier, inc=1, device_id={"tp": lax.rem(mt + k, T)}, device_id_type=MESH
        )

    for copy in small:
        copy.wait()
    row = lax.broadcasted_iota(jnp.int32, (16, HD), 0)
    sample = lax.rem(row, 4)

    def by_sample(values):
        return jnp.where(
            sample == 0,
            values[0],
            jnp.where(sample == 1, values[1], jnp.where(sample == 2, values[2], values[3])),
        )

    my_len = [len_s[0, me * 4 + i] for i in range(4)]
    my_div = [div_s[0, me * 4 + i] for i in range(4)]
    freq = tab_v[FREQ : FREQ + 1, :]
    q = q_v[...].astype(jnp.float32)
    q = jnp.concatenate([q[:, h * HD : (h + 1) * HD] for h in range(4)], axis=0)
    q_swapped = swap_halves(q)

    def rotate(positions):
        angle = by_sample(positions).astype(jnp.float32) * freq
        return (q * jnp.cos(angle) + q_swapped * jnp.sin(angle)).astype(jnp.bfloat16)

    q_app = rotate([my_len[i] - 128 * my_div[i] for i in range(4)])
    q_res[...] = rotate(my_len)
    q_send[...] = q_app
    q_all[me] = q_app

    pl.semaphore_wait(barrier, S - 1 + T - 1)

    @pl.loop(1, S)
    def _(k):
        pltpu.make_async_remote_copy(
            src_ref=q_send,
            dst_ref=q_all.at[me],
            send_sem=send_sem.at[0],
            recv_sem=recv_sem.at[0],
            device_id={"samp": lax.rem(me + k, S)},
            device_id_type=MESH,
        ).start()

    used = len_v[...] - 128 * div_v[...]
    high = lax.shift_right_logical(used, 7)
    low = used - 128 * high
    pair_row = lax.broadcasted_iota(jnp.int32, (16, 128), 0)
    pair = jnp.where(pair_row == 0, high, jnp.where(pair_row == 1, low, 0))
    e_row = lax.broadcasted_iota(jnp.int32, (128, 512), 0)
    e_col = lax.broadcasted_iota(jnp.int32, (128, 512), 1)
    spread = jnp.where(
        e_row == 4 * lax.shift_right_logical(e_col, 4) + jnp.bitwise_and(e_col, 3), 1.0, 0.0
    ).astype(jnp.bfloat16)
    wide = jnp.dot(
        pair.astype(jnp.float32).astype(jnp.bfloat16), spread, preferred_element_type=jnp.float32
    )
    used_wide = (wide[0:1] * 128.0 + wide[1:2]).astype(jnp.int32)

    p_row = lax.broadcasted_iota(jnp.int32, (256, 256), 0)
    p_col = lax.broadcasted_iota(jnp.int32, (256, 256), 1)
    perm = jnp.where(
        p_col == jnp.where(p_row < 128, 2 * p_row, 2 * p_row - 255), 1.0, 0.0
    ).astype(jnp.bfloat16)
    acc = jnp.zeros((ROWS, 256), jnp.float32)
    for c in range(NC):
        w_copies[c].wait()
        for i in range(c * DC // 256, (c + 1) * DC // 256):
            pairs = jnp.concatenate(
                [w_v[pl.ds(i * 512, 256), :], w_v[pl.ds(i * 512 + 256, 256), :]], axis=1
            )
            apart = jnp.dot(perm, pairs, preferred_element_type=jnp.float32).astype(jnp.bfloat16)
            wd[pl.ds(i * 256, 128), 0:128] = apart[0:128, 0:128]
            wd[pl.ds(i * 256, 128), 128:256] = apart[128:256, 0:128]
            wd[pl.ds(i * 256 + 128, 128), 0:128] = apart[0:128, 128:256]
            wd[pl.ds(i * 256 + 128, 128), 128:256] = apart[128:256, 128:256]
        x_copies[c].wait()
        acc = acc + jnp.dot(
            x_v[:, c * DC : (c + 1) * DC],
            wd[c * DC : (c + 1) * DC, :],
            preferred_element_type=jnp.float32,
        )
    raw = acc[:, 0:128]
    values = acc[:, 128:256].astype(jnp.bfloat16)
    scale = lax.rsqrt(jnp.mean(raw * raw, axis=1, keepdims=True) + NORM_EPS)
    keys = raw * scale * gain_v[...]
    cos_b = tab_v[pl.ds(COSB + me, 1), :]
    sin_b = tab_v[pl.ds(SINB + me, 1), :]
    cos_0 = tab_v[COS0 : COS0 + ROWS, :]
    sin_0 = tab_v[SIN0 : SIN0 + ROWS, :]
    cos = cos_0 * cos_b - sin_0 * sin_b
    sin = sin_0 * cos_b + cos_0 * sin_b
    keys = (keys * cos + swap_halves(keys) * sin).astype(jnp.bfloat16)

    pltpu.make_async_copy(
        q_all.at[pl.ds(0, S - 1)], q_all.at[pl.ds(0, S - 1)], recv_sem.at[0]
    ).wait()
    scores = lax.dot_general(
        keys,
        q_all[...].reshape(S * 16, HD),
        (((1,), (1,)), ((), ())),
        preferred_element_type=jnp.float32,
    ) * (HD**-0.5)
    position = lax.broadcasted_iota(jnp.int32, (ROWS, S * 16), 0) + me * ROWS
    valid = position < used_wide
    top = jnp.max(jnp.where(valid, scores, FLOOR), axis=0, keepdims=True)
    weights = jnp.where(valid, jnp.exp(scores - top), 0.0)
    total = jnp.sum(weights, axis=0, keepdims=True)
    part = lax.dot_general(
        weights.astype(jnp.bfloat16),
        values,
        (((0,), (0,)), ((), ())),
        preferred_element_type=jnp.float32,
    )
    o_send[...] = part.astype(jnp.bfloat16).reshape(S, 16, HD)
    for g in range(4):
        st_send[g, 0:1, :] = top[:, g * 128 : (g + 1) * 128]
        st_send[g, 1:2, :] = total[:, g * 128 : (g + 1) * 128]

    @pl.loop(1, S)
    def _(k):
        peer = lax.rem(me + k, S)
        pltpu.make_async_remote_copy(
            src_ref=o_send.at[peer],
            dst_ref=o_all.at[me],
            send_sem=send_sem.at[1],
            recv_sem=recv_sem.at[1],
            device_id={"samp": peer},
            device_id_type=MESH,
        ).start()
        pltpu.make_async_remote_copy(
            src_ref=st_send.at[peer // 8],
            dst_ref=st_all.at[me],
            send_sem=send_sem.at[2],
            recv_sem=recv_sem.at[2],
            device_id={"samp": peer},
            device_id_type=MESH,
        ).start()

    o_all[me] = o_send[me]
    st_all[me] = st_send[me // 8]

    for copy in pages:
        copy.wait()
    lane = lax.broadcasted_iota(jnp.int32, (16, HD), 1)
    slot_ok = jnp.zeros((16, HD), jnp.float32)
    for j in range(4):
        page = by_sample([pt_s[i, j] for i in range(4)])
        count = by_sample(my_div)
        slot_ok = jnp.where((lane == page) & (count > j), 1.0, slot_ok)
    seen = jnp.concatenate(
        [jnp.broadcast_to(slot_ok[:, k : k + 1], (16, HD)) for k in range(16)], axis=1
    ) > 0.5
    res_scores = lax.dot_general(
        q_res[...], rk_v[...], (((1,), (1,)), ((), ())), preferred_element_type=jnp.float32
    ) * (HD**-0.5)
    res_top = jnp.max(jnp.where(seen, res_scores, FLOOR), axis=1, keepdims=True)
    res_weights = jnp.where(seen, jnp.exp(res_scores - res_top), 0.0)
    res_total = jnp.sum(res_weights, axis=1, keepdims=True)
    res_part = jnp.dot(
        res_weights.astype(jnp.bfloat16), rv_v[...], preferred_element_type=jnp.float32
    )

    pltpu.make_async_copy(
        st_all.at[pl.ds(0, S - 1)], st_all.at[pl.ds(0, S - 1)], recv_sem.at[2]
    ).wait()
    pltpu.make_async_copy(
        o_all.at[pl.ds(0, S - 1)], o_all.at[pl.ds(0, S - 1)], recv_sem.at[1]
    ).wait()
    tops = jnp.concatenate([st_all[:, 0, :], jnp.full((128 - S, 128), FLOOR, jnp.float32)], axis=0)
    totals = jnp.concatenate([st_all[:, 1, :], jnp.zeros((128 - S, 128), jnp.float32)], axis=0)
    tr_v[0] = tops.T
    tr_v[1] = totals.T
    mine = pl.multiple_of(16 * lax.rem(me, 8), 16)
    tops = tr_v[0, pl.ds(mine, 16), :]
    totals = tr_v[1, pl.ds(mine, 16), :]
    highest = jnp.maximum(jnp.max(tops, axis=1, keepdims=True), res_top)
    factor = jnp.exp(tops - highest)
    res_factor = jnp.exp(res_top - highest)
    whole = jnp.sum(factor * totals, axis=1, keepdims=True) + res_factor * res_total
    attended = res_part * res_factor
    for i in range(S):
        attended = attended + factor[:, i : i + 1] * o_all[i].astype(jnp.float32)
    attended = attended / whole
    attended = jnp.concatenate(
        [attended if h == 0 else pltpu.roll(attended, 16 - 4 * h, 0) for h in range(4)], axis=1
    ).astype(jnp.bfloat16)

    ow_copy.wait()

    @pl.loop(1, T)
    def _(k):
        peer = lax.rem(mt + k, T)
        columns = pl.ds(pl.multiple_of(peer * COLS, COLS), COLS)
        piece = jnp.dot(attended, ow_v[:, columns], preferred_element_type=jnp.float32)
        rs_send[peer] = piece[0:4, :]
        pltpu.make_async_remote_copy(
            src_ref=rs_send.at[peer],
            dst_ref=rs_all.at[mt],
            send_sem=send_sem.at[3],
            recv_sem=recv_sem.at[3],
            device_id={"tp": peer},
            device_id_type=MESH,
        ).start()

    columns = pl.ds(pl.multiple_of(mt * COLS, COLS), COLS)
    rs_all[mt] = jnp.dot(attended, ow_v[:, columns], preferred_element_type=jnp.float32)[0:4, :]
    pltpu.make_async_copy(
        rs_all.at[pl.ds(0, T - 1)], rs_all.at[pl.ds(0, T - 1)], recv_sem.at[3]
    ).wait()
    piece = rs_all[0]
    for t in range(1, T):
        piece = piece + rs_all[t]
    ag[mt] = piece

    @pl.loop(1, T)
    def _(k):
        pltpu.make_async_remote_copy(
            src_ref=ag.at[mt],
            dst_ref=ag.at[mt],
            send_sem=send_sem.at[4],
            recv_sem=recv_sem.at[4],
            device_id={"tp": lax.rem(mt + k, T)},
            device_id_type=MESH,
        ).start()

    pltpu.make_async_copy(
        ag.at[pl.ds(0, T - 1)], ag.at[pl.ds(0, T - 1)], recv_sem.at[4]
    ).wait()
    for t in range(T):
        out_ref[:, t * COLS : (t + 1) * COLS] = ag[t].astype(jnp.bfloat16)

    for sem, buffer, n in ((0, q_all, S), (1, o_all, S), (2, st_all, S), (3, rs_all, T), (4, ag, T)):
        part_ref = buffer.at[pl.ds(0, n - 1)]
        pltpu.make_async_copy(part_ref, part_ref, send_sem.at[sem]).wait()


def local(x, w, gain, q, rk, rv, pt, div, length, ow):
    bf16, f32, i32 = jnp.bfloat16, jnp.float32, jnp.int32
    hbm = pl.BlockSpec(memory_space=pl.ANY)
    V = pltpu.VMEM
    return pl.pallas_call(
        kernel,
        out_shape=jax.ShapeDtypeStruct((4, D), bf16),
        in_specs=[hbm] * 11,
        out_specs=pl.BlockSpec(memory_space=pltpu.VMEM),
        scratch_shapes=[
            V((ROWS, D), bf16),
            V((2 * D, HD), bf16),
            V((D, 256), bf16),
            V((1, HD), f32),
            V((4, 512), bf16),
            V((2048, HD), bf16),
            V((2048, HD), bf16),
            pltpu.SMEM((4, 4), i32),
            pltpu.SMEM((1, 128), i32),
            pltpu.SMEM((1, 128), i32),
            V((1, 128), i32),
            V((1, 128), i32),
            V((512, D), bf16),
            V((584, HD), f32),
            V((16, HD), bf16),
            V((16, HD), bf16),
            V((S, 16, HD), bf16),
            V((S, 16, HD), bf16),
            V((S, 16, HD), bf16),
            V((4, 2, 128), f32),
            V((S, 2, 128), f32),
            V((2, 128, 128), f32),
            V((T, 4, COLS), f32),
            V((T, 4, COLS), f32),
            V((T, 4, COLS), f32),
            pltpu.SemaphoreType.DMA((8,)),
            pltpu.SemaphoreType.DMA((2, NC)),
            pltpu.SemaphoreType.DMA((2,)),
            pltpu.SemaphoreType.DMA,
            pltpu.SemaphoreType.DMA((5,)),
            pltpu.SemaphoreType.DMA((5,)),
        ],
        compiler_params=pltpu.CompilerParams(
            collective_id=0, has_side_effects=True, vmem_limit_bytes=62 * 1024 * 1024
        ),
        cost_estimate=pl.CostEstimate(
            flops=1_500_000_000, bytes_accessed=12_000_000, transcendentals=200_000
        ),
    )(
        x,
        w.reshape(2 * D, HD),
        gain.reshape(1, HD),
        q,
        rk.reshape(2048, HD),
        rv.reshape(2048, HD),
        pt,
        div.reshape(1, 128),
        length.reshape(1, 128),
        ow,
        jnp.asarray(rope_table()),
    )


def solution(mesh):
    return jax.shard_map(
        local,
        mesh=mesh,
        in_specs=(
            P("samp", None),
            P(None, None, "tp"),
            P(),
            P("samp", "tp"),
            P("samp", None, "tp"),
            P("samp", None, "tp"),
            P("samp", None),
            P(),
            P(),
            P("tp", None),
        ),
        out_specs=P("samp", None),
        check_vma=False,
    )
```

```python
import numpy as np
import jax
import jax.numpy as jnp
from jax import lax
from jax.experimental import pallas as pl
from jax.experimental.pallas import tpu as pltpu
from jax.sharding import PartitionSpec as P

ROPE_BASE = 1000000.0
NORM_EPS = 1e-06
FLOOR = -1e30
S = 32
T = 8
HD = 128
D = 5120
ROWS = 256
NC = 5
DC = D // NC
COL4 = D // 4
PC = 256
NP = COL4 // PC
MESH = pl.DeviceIdType.MESH

COS0, SIN0, COSB, SINB, FREQ = 0, 256, 512, 544, 576


def rope_table():
    freq = ROPE_BASE ** (-(np.arange(64, dtype=np.float64) * 2.0 / HD))
    freq = np.concatenate([freq, freq])
    row = np.arange(ROWS, dtype=np.float64)[:, None] * freq
    base = (np.arange(S, dtype=np.float64) * ROWS)[:, None] * freq
    last = np.zeros((8, HD))
    last[:] = freq
    return np.concatenate([np.cos(row), np.sin(row), np.cos(base), np.sin(base), last]).astype(
        np.float32
    )


def samp_peer(me, k):
    dz, dx = k // 4, k % 4
    dz = 4 + (dz + 1) // 2 * (1 - 2 * (dz % 2))
    dx = 2 + (dx + 1) // 2 * (1 - 2 * (dx % 2))
    return lax.rem(me // 8 + dx, 4) * 8 + lax.rem(lax.rem(me, 8) + dz, 8)


def tp_peers(mt):
    for dy in (2, 1, 3, 0):
        same = lax.rem(mt + 2 * dy, T)
        if dy:
            yield same
        yield same + 1 - 2 * lax.rem(same, 2)


def swap_halves(v):
    lane = lax.broadcasted_iota(jnp.int32, v.shape, 1)
    return jnp.where(lane < 64, -1.0, 1.0) * pltpu.roll(v, 64, 1)


def kernel(
    x_hbm,
    w_hbm,
    gain_hbm,
    q_hbm,
    rk_hbm,
    rv_hbm,
    pt_hbm,
    div_hbm,
    len_hbm,
    ow_hbm,
    tab_hbm,
    out_ref,
    x_v,
    w_v,
    wd,
    gain_v,
    q_v,
    rk_v,
    rv_v,
    pt_s,
    div_s,
    len_s,
    div_v,
    len_v,
    ow_v,
    tab_v,
    q_send,
    q_res,
    q_all,
    o_send,
    o_all,
    st_send,
    st_all,
    tr_v,
    tp_send,
    tp_all,
    small_sem,
    chunk_sem,
    page_sem,
    ow_sem,
    send_sem,
    recv_sem,
):
    me = lax.axis_index("samp")
    mt = lax.axis_index("tp")

    small = [
        pltpu.make_async_copy(src, dst, small_sem.at[i])
        for i, (src, dst) in enumerate(
            [
                (len_hbm, len_s),
                (div_hbm, div_s),
                (q_hbm, q_v),
                (tab_hbm, tab_v),
                (pt_hbm, pt_s),
                (len_hbm, len_v),
                (div_hbm, div_v),
                (gain_hbm, gain_v),
            ]
        )
    ]
    for copy in small:
        copy.start()
    w_copies = [
        pltpu.make_async_copy(
            w_hbm.at[pl.ds(c * 2 * DC, 2 * DC)], w_v.at[pl.ds(c * 2 * DC, 2 * DC)], chunk_sem.at[0, c]
        )
        for c in range(NC)
    ]
    x_copies = [
        pltpu.make_async_copy(
            x_hbm.at[:, pl.ds(c * DC, DC)], x_v.at[:, pl.ds(c * DC, DC)], chunk_sem.at[1, c]
        )
        for c in range(NC)
    ]
    for c in range(NC):
        w_copies[c].start()
        x_copies[c].start()
    pages = [
        pltpu.make_async_copy(rk_hbm, rk_v, page_sem.at[0]),
        pltpu.make_async_copy(rv_hbm, rv_v, page_sem.at[1]),
    ]
    for copy in pages:
        copy.start()
    ow_copy = pltpu.make_async_copy(ow_hbm, ow_v, ow_sem)
    ow_copy.start()

    barrier = pltpu.get_barrier_semaphore()

    @pl.loop(0, S - 1)
    def _(k):
        pl.semaphore_signal(
            barrier, inc=1, device_id={"samp": samp_peer(me, k)}, device_id_type=MESH
        )

    for peer in tp_peers(mt):
        pl.semaphore_signal(barrier, inc=1, device_id={"tp": peer}, device_id_type=MESH)

    for copy in small:
        copy.wait()
    row = lax.broadcasted_iota(jnp.int32, (16, HD), 0)
    sample = lax.rem(row, 4)

    def by_sample(values):
        return jnp.where(
            sample == 0,
            values[0],
            jnp.where(sample == 1, values[1], jnp.where(sample == 2, values[2], values[3])),
        )

    my_len = [len_s[0, me * 4 + i] for i in range(4)]
    my_div = [div_s[0, me * 4 + i] for i in range(4)]
    freq = tab_v[FREQ : FREQ + 1, :]
    q = q_v[...].astype(jnp.float32)
    q = jnp.concatenate([q[:, h * HD : (h + 1) * HD] for h in range(4)], axis=0)
    q_swapped = swap_halves(q)

    def rotate(positions):
        angle = by_sample(positions).astype(jnp.float32) * freq
        return (q * jnp.cos(angle) + q_swapped * jnp.sin(angle)).astype(jnp.bfloat16)

    q_app = rotate([my_len[i] - 128 * my_div[i] for i in range(4)])
    q_res[...] = rotate(my_len)
    q_send[...] = q_app
    q_all[me] = q_app

    pl.semaphore_wait(barrier, S - 1 + T - 1)

    @pl.loop(0, S - 1)
    def _(k):
        pltpu.make_async_remote_copy(
            src_ref=q_send,
            dst_ref=q_all.at[me],
            send_sem=send_sem.at[0],
            recv_sem=recv_sem.at[0],
            device_id={"samp": samp_peer(me, k)},
            device_id_type=MESH,
        ).start()

    used = len_v[...] - 128 * div_v[...]
    high = lax.shift_right_logical(used, 7)
    low = used - 128 * high
    pair_row = lax.broadcasted_iota(jnp.int32, (16, 128), 0)
    pair = jnp.where(pair_row == 0, high, jnp.where(pair_row == 1, low, 0))
    e_row = lax.broadcasted_iota(jnp.int32, (128, 512), 0)
    e_col = lax.broadcasted_iota(jnp.int32, (128, 512), 1)
    spread = jnp.where(
        e_row == 4 * lax.shift_right_logical(e_col, 4) + jnp.bitwise_and(e_col, 3), 1.0, 0.0
    ).astype(jnp.bfloat16)
    wide = jnp.dot(
        pair.astype(jnp.float32).astype(jnp.bfloat16), spread, preferred_element_type=jnp.float32
    )
    used_wide = (wide[0:1] * 128.0 + wide[1:2]).astype(jnp.int32)

    p_row = lax.broadcasted_iota(jnp.int32, (256, 256), 0)
    p_col = lax.broadcasted_iota(jnp.int32, (256, 256), 1)
    perm = jnp.where(
        p_col == jnp.where(p_row < 128, 2 * p_row, 2 * p_row - 255), 1.0, 0.0
    ).astype(jnp.bfloat16)
    acc = jnp.zeros((ROWS, 256), jnp.float32)
    for c in range(NC):
        w_copies[c].wait()
        for i in range(c * DC // 256, (c + 1) * DC // 256):
            pairs = jnp.concatenate(
                [w_v[pl.ds(i * 512, 256), :], w_v[pl.ds(i * 512 + 256, 256), :]], axis=1
            )
            apart = jnp.dot(perm, pairs, preferred_element_type=jnp.float32).astype(jnp.bfloat16)
            wd[pl.ds(i * 256, 128), 0:128] = apart[0:128, 0:128]
            wd[pl.ds(i * 256, 128), 128:256] = apart[128:256, 0:128]
            wd[pl.ds(i * 256 + 128, 128), 0:128] = apart[0:128, 128:256]
            wd[pl.ds(i * 256 + 128, 128), 128:256] = apart[128:256, 128:256]
        x_copies[c].wait()
        acc = acc + jnp.dot(
            x_v[:, c * DC : (c + 1) * DC],
            wd[c * DC : (c + 1) * DC, :],
            preferred_element_type=jnp.float32,
        )
    raw = acc[:, 0:128]
    values = acc[:, 128:256].astype(jnp.bfloat16)
    scale = lax.rsqrt(jnp.mean(raw * raw, axis=1, keepdims=True) + NORM_EPS)
    keys = raw * scale * gain_v[...]
    cos_b = tab_v[pl.ds(COSB + me, 1), :]
    sin_b = tab_v[pl.ds(SINB + me, 1), :]
    cos_0 = tab_v[COS0 : COS0 + ROWS, :]
    sin_0 = tab_v[SIN0 : SIN0 + ROWS, :]
    cos = cos_0 * cos_b - sin_0 * sin_b
    sin = sin_0 * cos_b + cos_0 * sin_b
    keys = (keys * cos + swap_halves(keys) * sin).astype(jnp.bfloat16)

    pltpu.make_async_copy(
        q_all.at[pl.ds(0, S - 1)], q_all.at[pl.ds(0, S - 1)], recv_sem.at[0]
    ).wait()
    scores = lax.dot_general(
        keys,
        q_all[...].reshape(S * 16, HD),
        (((1,), (1,)), ((), ())),
        preferred_element_type=jnp.float32,
    ) * (HD**-0.5)
    position = lax.broadcasted_iota(jnp.int32, (ROWS, S * 16), 0) + me * ROWS
    valid = position < used_wide
    top = jnp.max(jnp.where(valid, scores, FLOOR), axis=0, keepdims=True)
    weights = jnp.where(valid, jnp.exp(scores - top), 0.0)
    total = jnp.sum(weights, axis=0, keepdims=True)
    part = lax.dot_general(
        weights.astype(jnp.bfloat16),
        values,
        (((0,), (0,)), ((), ())),
        preferred_element_type=jnp.float32,
    )
    o_send[...] = part.astype(jnp.bfloat16).reshape(S, 16, HD)
    for g in range(4):
        st_send[g, 0:1, :] = top[:, g * 128 : (g + 1) * 128]
        st_send[g, 1:2, :] = total[:, g * 128 : (g + 1) * 128]

    @pl.loop(0, S - 1)
    def _(k):
        peer = samp_peer(me, k)
        pltpu.make_async_remote_copy(
            src_ref=o_send.at[peer],
            dst_ref=o_all.at[me],
            send_sem=send_sem.at[1],
            recv_sem=recv_sem.at[1],
            device_id={"samp": peer},
            device_id_type=MESH,
        ).start()
        pltpu.make_async_remote_copy(
            src_ref=st_send.at[peer // 8],
            dst_ref=st_all.at[me],
            send_sem=send_sem.at[2],
            recv_sem=recv_sem.at[2],
            device_id={"samp": peer},
            device_id_type=MESH,
        ).start()

    o_all[me] = o_send[me]
    st_all[me] = st_send[me // 8]

    for copy in pages:
        copy.wait()
    lane = lax.broadcasted_iota(jnp.int32, (16, HD), 1)
    slot_ok = jnp.zeros((16, HD), jnp.float32)
    for j in range(4):
        page = by_sample([pt_s[i, j] for i in range(4)])
        count = by_sample(my_div)
        slot_ok = jnp.where((lane == page) & (count > j), 1.0, slot_ok)
    seen = jnp.concatenate(
        [jnp.broadcast_to(slot_ok[:, k : k + 1], (16, HD)) for k in range(16)], axis=1
    ) > 0.5
    res_scores = lax.dot_general(
        q_res[...], rk_v[...], (((1,), (1,)), ((), ())), preferred_element_type=jnp.float32
    ) * (HD**-0.5)
    res_top = jnp.max(jnp.where(seen, res_scores, FLOOR), axis=1, keepdims=True)
    res_weights = jnp.where(seen, jnp.exp(res_scores - res_top), 0.0)
    res_total = jnp.sum(res_weights, axis=1, keepdims=True)
    res_part = jnp.dot(
        res_weights.astype(jnp.bfloat16), rv_v[...], preferred_element_type=jnp.float32
    )

    pltpu.make_async_copy(
        st_all.at[pl.ds(0, S - 1)], st_all.at[pl.ds(0, S - 1)], recv_sem.at[2]
    ).wait()
    pltpu.make_async_copy(
        o_all.at[pl.ds(0, S - 1)], o_all.at[pl.ds(0, S - 1)], recv_sem.at[1]
    ).wait()
    tops = jnp.concatenate([st_all[:, 0, :], jnp.full((128 - S, 128), FLOOR, jnp.float32)], axis=0)
    totals = jnp.concatenate([st_all[:, 1, :], jnp.zeros((128 - S, 128), jnp.float32)], axis=0)
    tr_v[0] = tops.T
    tr_v[1] = totals.T
    mine = pl.multiple_of(16 * lax.rem(me, 8), 16)
    tops = tr_v[0, pl.ds(mine, 16), :]
    totals = tr_v[1, pl.ds(mine, 16), :]
    highest = jnp.maximum(jnp.max(tops, axis=1, keepdims=True), res_top)
    factor = jnp.exp(tops - highest)
    res_factor = jnp.exp(res_top - highest)
    whole = jnp.sum(factor * totals, axis=1, keepdims=True) + res_factor * res_total
    attended = res_part * res_factor
    for i in range(S):
        attended = attended + factor[:, i : i + 1] * o_all[i].astype(jnp.float32)
    attended = attended / whole
    turned = [attended] + [pltpu.roll(attended, 4 * n, 0) for n in range(1, 4)]

    ow_copy.wait()
    group = lax.shift_right_logical(lax.broadcasted_iota(jnp.int32, (16, 512), 0), 2)
    placed = [
        jnp.where(
            group == c, jnp.concatenate([turned[(c - h) % 4] for h in range(4)], axis=1), 0.0
        ).astype(jnp.bfloat16)
        for c in range(4)
    ]
    for p in range(NP):
        share = sum(
            jnp.dot(
                placed[c],
                ow_v[:, COL4 * c + PC * p : COL4 * c + PC * (p + 1)],
                preferred_element_type=jnp.float32,
            )
            for c in range(4)
        ).astype(jnp.bfloat16)
        tp_send[p] = share
        for peer in tp_peers(mt):
            pltpu.make_async_remote_copy(
                src_ref=tp_send.at[p],
                dst_ref=tp_all.at[mt, p],
                send_sem=send_sem.at[3],
                recv_sem=recv_sem.at[3],
                device_id={"tp": peer},
                device_id_type=MESH,
            ).start()
        tp_all[mt, p] = share
    pltpu.make_async_copy(
        tp_all.at[pl.ds(0, T - 1)], tp_all.at[pl.ds(0, T - 1)], recv_sem.at[3]
    ).wait()
    for p in range(NP):
        mixed = sum(tp_all[t, p].astype(jnp.float32) for t in range(T))
        for c in range(4):
            out_ref[:, COL4 * c + PC * p : COL4 * c + PC * (p + 1)] = mixed[
                4 * c : 4 * c + 4, :
            ].astype(jnp.bfloat16)

    for sem, buffer, n in ((0, q_all, S), (1, o_all, S), (2, st_all, S), (3, tp_all, T)):
        part_ref = buffer.at[pl.ds(0, n - 1)]
        pltpu.make_async_copy(part_ref, part_ref, send_sem.at[sem]).wait()


def local(x, w, gain, q, rk, rv, pt, div, length, ow):
    bf16, f32, i32 = jnp.bfloat16, jnp.float32, jnp.int32
    hbm = pl.BlockSpec(memory_space=pl.ANY)
    V = pltpu.VMEM
    return pl.pallas_call(
        kernel,
        out_shape=jax.ShapeDtypeStruct((4, D), bf16),
        in_specs=[hbm] * 11,
        out_specs=pl.BlockSpec(memory_space=pltpu.VMEM),
        scratch_shapes=[
            V((ROWS, D), bf16),
            V((2 * D, HD), bf16),
            V((D, 256), bf16),
            V((1, HD), f32),
            V((4, 512), bf16),
            V((2048, HD), bf16),
            V((2048, HD), bf16),
            pltpu.SMEM((4, 4), i32),
            pltpu.SMEM((1, 128), i32),
            pltpu.SMEM((1, 128), i32),
            V((1, 128), i32),
            V((1, 128), i32),
            V((512, D), bf16),
            V((584, HD), f32),
            V((16, HD), bf16),
            V((16, HD), bf16),
            V((S, 16, HD), bf16),
            V((S, 16, HD), bf16),
            V((S, 16, HD), bf16),
            V((4, 2, 128), f32),
            V((S, 2, 128), f32),
            V((2, 128, 128), f32),
            V((NP, 16, PC), bf16),
            V((T, NP, 16, PC), bf16),
            pltpu.SemaphoreType.DMA((8,)),
            pltpu.SemaphoreType.DMA((2, NC)),
            pltpu.SemaphoreType.DMA((2,)),
            pltpu.SemaphoreType.DMA,
            pltpu.SemaphoreType.DMA((4,)),
            pltpu.SemaphoreType.DMA((4,)),
        ],
        compiler_params=pltpu.CompilerParams(
            collective_id=0, has_side_effects=True, vmem_limit_bytes=62 * 1024 * 1024
        ),
        cost_estimate=pl.CostEstimate(
            flops=1_500_000_000, bytes_accessed=12_000_000, transcendentals=200_000
        ),
    )(
        x,
        w.reshape(2 * D, HD),
        gain.reshape(1, HD),
        q,
        rk.reshape(2048, HD),
        rv.reshape(2048, HD),
        pt,
        div.reshape(1, 128),
        length.reshape(1, 128),
        ow,
        jnp.asarray(rope_table()),
    )


def solution(mesh):
    return jax.shard_map(
        local,
        mesh=mesh,
        in_specs=(
            P("samp", None),
            P(None, None, "tp"),
            P(),
            P("samp", "tp"),
            P("samp", None, "tp"),
            P("samp", None, "tp"),
            P("samp", None),
            P(),
            P(),
            P("tp", None),
        ),
        out_specs=P("samp", None),
        check_vma=False,
    )
```

```python
import numpy as np
import jax
import jax.numpy as jnp
from jax import lax
from jax.experimental import pallas as pl
from jax.experimental.pallas import tpu as pltpu
from jax.sharding import PartitionSpec as P

ROPE_BASE = 1000000.0
NORM_EPS = 1e-06
FLOOR = -1e30
S = 32
T = 8
HD = 128
D = 5120
ROWS = 256
NC = 5
DC = D // NC
COL4 = D // 4
PC = 256
NP = COL4 // PC
MESH = pl.DeviceIdType.MESH

COS0, SIN0, COSB, SINB, FREQ = 0, 256, 512, 544, 576


def rope_table():
    freq = ROPE_BASE ** (-(np.arange(64, dtype=np.float64) * 2.0 / HD))
    freq = np.concatenate([freq, freq])
    row = np.arange(ROWS, dtype=np.float64)[:, None] * freq
    base = (np.arange(S, dtype=np.float64) * ROWS)[:, None] * freq
    last = np.zeros((8, HD))
    last[:] = freq
    return np.concatenate([np.cos(row), np.sin(row), np.cos(base), np.sin(base), last]).astype(
        np.float32
    )


def samp_peer(me, k):
    dz, dx = k // 4, k % 4
    dz = 4 + (dz + 1) // 2 * (1 - 2 * (dz % 2))
    dx = 2 + (dx + 1) // 2 * (1 - 2 * (dx % 2))
    return lax.rem(me // 8 + dx, 4) * 8 + lax.rem(lax.rem(me, 8) + dz, 8)


def tp_peers(mt):
    for dy in (2, 1, 3, 0):
        same = lax.rem(mt + 2 * dy, T)
        if dy:
            yield same
        yield same + 1 - 2 * lax.rem(same, 2)


def swap_halves(v):
    lane = lax.broadcasted_iota(jnp.int32, v.shape, 1)
    return jnp.where(lane < 64, -1.0, 1.0) * pltpu.roll(v, 64, 1)


def kernel(
    x_hbm,
    w_hbm,
    gain_hbm,
    q_hbm,
    rk_hbm,
    rv_hbm,
    pt_hbm,
    div_hbm,
    len_hbm,
    ow_hbm,
    tab_hbm,
    out_ref,
    x_v,
    w_v,
    wd,
    gain_v,
    q_v,
    rk_v,
    rv_v,
    pt_s,
    div_s,
    len_s,
    div_v,
    len_v,
    ow_v,
    tab_v,
    q_send,
    q_res,
    q_all,
    o_send,
    o_all,
    st_send,
    st_all,
    tr_v,
    tp_send,
    tp_all,
    small_sem,
    chunk_sem,
    page_sem,
    ow_sem,
    send_sem,
    recv_sem,
):
    me = lax.axis_index("samp")
    mt = lax.axis_index("tp")

    small = [
        pltpu.make_async_copy(src, dst, small_sem.at[i])
        for i, (src, dst) in enumerate(
            [
                (len_hbm, len_s),
                (div_hbm, div_s),
                (q_hbm, q_v),
                (tab_hbm, tab_v),
                (pt_hbm, pt_s),
                (len_hbm, len_v),
                (div_hbm, div_v),
                (gain_hbm, gain_v),
            ]
        )
    ]
    for copy in small:
        copy.start()
    w_copies = [
        pltpu.make_async_copy(
            w_hbm.at[pl.ds(c * 2 * DC, 2 * DC)], w_v.at[pl.ds(c * 2 * DC, 2 * DC)], chunk_sem.at[0, c]
        )
        for c in range(NC)
    ]
    x_copies = [
        pltpu.make_async_copy(
            x_hbm.at[:, pl.ds(c * DC, DC)], x_v.at[:, pl.ds(c * DC, DC)], chunk_sem.at[1, c]
        )
        for c in range(NC)
    ]
    for c in range(NC):
        w_copies[c].start()
        x_copies[c].start()
    pages = [
        pltpu.make_async_copy(rk_hbm, rk_v, page_sem.at[0]),
        pltpu.make_async_copy(rv_hbm, rv_v, page_sem.at[1]),
    ]
    for copy in pages:
        copy.start()
    ow_copy = pltpu.make_async_copy(ow_hbm, ow_v, ow_sem)
    ow_copy.start()

    barrier = pltpu.get_barrier_semaphore()

    @pl.loop(0, S - 1)
    def _(k):
        pl.semaphore_signal(
            barrier, inc=1, device_id={"samp": samp_peer(me, k)}, device_id_type=MESH
        )

    for peer in tp_peers(mt):
        pl.semaphore_signal(barrier, inc=1, device_id={"tp": peer}, device_id_type=MESH)

    for copy in small:
        copy.wait()
    row = lax.broadcasted_iota(jnp.int32, (16, HD), 0)
    sample = lax.rem(row, 4)

    def by_sample(values):
        return jnp.where(
            sample == 0,
            values[0],
            jnp.where(sample == 1, values[1], jnp.where(sample == 2, values[2], values[3])),
        )

    my_len = [len_s[0, me * 4 + i] for i in range(4)]
    my_div = [div_s[0, me * 4 + i] for i in range(4)]
    freq = tab_v[FREQ : FREQ + 1, :]
    q = q_v[...].astype(jnp.float32)
    q = jnp.concatenate([q[:, h * HD : (h + 1) * HD] for h in range(4)], axis=0)
    q_swapped = swap_halves(q)

    def rotate(positions):
        angle = by_sample(positions).astype(jnp.float32) * freq
        return (q * jnp.cos(angle) + q_swapped * jnp.sin(angle)).astype(jnp.bfloat16)

    q_app = rotate([my_len[i] - 128 * my_div[i] for i in range(4)])
    q_res[...] = rotate(my_len)
    q_send[...] = q_app
    q_all[me] = q_app

    pl.semaphore_wait(barrier, S - 1 + T - 1)

    @pl.loop(0, S - 1)
    def _(k):
        pltpu.make_async_remote_copy(
            src_ref=q_send,
            dst_ref=q_all.at[me],
            send_sem=send_sem.at[0],
            recv_sem=recv_sem.at[0],
            device_id={"samp": samp_peer(me, k)},
            device_id_type=MESH,
        ).start()

    used = len_v[...] - 128 * div_v[...]
    high = lax.shift_right_logical(used, 7)
    low = used - 128 * high
    pair_row = lax.broadcasted_iota(jnp.int32, (16, 128), 0)
    pair = jnp.where(pair_row == 0, high, jnp.where(pair_row == 1, low, 0))
    e_row = lax.broadcasted_iota(jnp.int32, (128, 512), 0)
    e_col = lax.broadcasted_iota(jnp.int32, (128, 512), 1)
    spread = jnp.where(
        e_row == 4 * lax.shift_right_logical(e_col, 4) + jnp.bitwise_and(e_col, 3), 1.0, 0.0
    ).astype(jnp.bfloat16)
    wide = jnp.dot(
        pair.astype(jnp.float32).astype(jnp.bfloat16), spread, preferred_element_type=jnp.float32
    )
    used_wide = (wide[0:1] * 128.0 + wide[1:2]).astype(jnp.int32)

    p_row = lax.broadcasted_iota(jnp.int32, (256, 256), 0)
    p_col = lax.broadcasted_iota(jnp.int32, (256, 256), 1)
    perm = jnp.where(
        p_col == jnp.where(p_row < 128, 2 * p_row, 2 * p_row - 255), 1.0, 0.0
    ).astype(jnp.bfloat16)
    acc = jnp.zeros((ROWS, 256), jnp.float32)
    for c in range(NC):
        w_copies[c].wait()
        for i in range(c * DC // 256, (c + 1) * DC // 256):
            pairs = jnp.concatenate(
                [w_v[pl.ds(i * 512, 256), :], w_v[pl.ds(i * 512 + 256, 256), :]], axis=1
            )
            apart = jnp.dot(perm, pairs, preferred_element_type=jnp.float32).astype(jnp.bfloat16)
            wd[pl.ds(i * 256, 128), 0:128] = apart[0:128, 0:128]
            wd[pl.ds(i * 256, 128), 128:256] = apart[128:256, 0:128]
            wd[pl.ds(i * 256 + 128, 128), 0:128] = apart[0:128, 128:256]
            wd[pl.ds(i * 256 + 128, 128), 128:256] = apart[128:256, 128:256]
        x_copies[c].wait()
        acc = acc + jnp.dot(
            x_v[:, c * DC : (c + 1) * DC],
            wd[c * DC : (c + 1) * DC, :],
            preferred_element_type=jnp.float32,
        )
    raw = acc[:, 0:128]
    values = acc[:, 128:256].astype(jnp.bfloat16)
    scale = lax.rsqrt(jnp.mean(raw * raw, axis=1, keepdims=True) + NORM_EPS)
    keys = raw * scale * gain_v[...]
    cos_b = tab_v[pl.ds(COSB + me, 1), :]
    sin_b = tab_v[pl.ds(SINB + me, 1), :]
    cos_0 = tab_v[COS0 : COS0 + ROWS, :]
    sin_0 = tab_v[SIN0 : SIN0 + ROWS, :]
    cos = cos_0 * cos_b - sin_0 * sin_b
    sin = sin_0 * cos_b + cos_0 * sin_b
    keys = (keys * cos + swap_halves(keys) * sin).astype(jnp.bfloat16)

    pltpu.make_async_copy(
        q_all.at[pl.ds(0, S - 1)], q_all.at[pl.ds(0, S - 1)], recv_sem.at[0]
    ).wait()
    scores = lax.dot_general(
        keys,
        q_all[...].reshape(S * 16, HD),
        (((1,), (1,)), ((), ())),
        preferred_element_type=jnp.float32,
    ) * (HD**-0.5)
    position = lax.broadcasted_iota(jnp.int32, (ROWS, S * 16), 0) + me * ROWS
    valid = position < used_wide
    top = jnp.max(jnp.where(valid, scores, FLOOR), axis=0, keepdims=True)
    weights = jnp.where(valid, jnp.exp(scores - top), 0.0)
    total = jnp.sum(weights, axis=0, keepdims=True)
    part = lax.dot_general(
        weights.astype(jnp.bfloat16),
        values,
        (((0,), (0,)), ((), ())),
        preferred_element_type=jnp.float32,
    )
    o_send[...] = part.astype(jnp.bfloat16).reshape(S, 16, HD)
    for g in range(4):
        st_send[g, 0:1, :] = top[:, g * 128 : (g + 1) * 128]
        st_send[g, 1:2, :] = total[:, g * 128 : (g + 1) * 128]

    @pl.loop(0, S - 1)
    def _(k):
        peer = samp_peer(me, k)
        pltpu.make_async_remote_copy(
            src_ref=o_send.at[peer],
            dst_ref=o_all.at[me],
            send_sem=send_sem.at[1],
            recv_sem=recv_sem.at[1],
            device_id={"samp": peer},
            device_id_type=MESH,
        ).start()
        pltpu.make_async_remote_copy(
            src_ref=st_send.at[peer // 8],
            dst_ref=st_all.at[me],
            send_sem=send_sem.at[2],
            recv_sem=recv_sem.at[2],
            device_id={"samp": peer},
            device_id_type=MESH,
        ).start()

    o_all[me] = o_send[me]
    st_all[me] = st_send[me // 8]

    for copy in pages:
        copy.wait()
    lane = lax.broadcasted_iota(jnp.int32, (16, HD), 1)
    slot_ok = jnp.zeros((16, HD), jnp.float32)
    for j in range(4):
        page = by_sample([pt_s[i, j] for i in range(4)])
        count = by_sample(my_div)
        slot_ok = jnp.where((lane == page) & (count > j), 1.0, slot_ok)
    seen = jnp.concatenate(
        [jnp.broadcast_to(slot_ok[:, k : k + 1], (16, HD)) for k in range(16)], axis=1
    ) > 0.5
    res_scores = lax.dot_general(
        q_res[...], rk_v[...], (((1,), (1,)), ((), ())), preferred_element_type=jnp.float32
    ) * (HD**-0.5)
    res_top = jnp.max(jnp.where(seen, res_scores, FLOOR), axis=1, keepdims=True)
    res_weights = jnp.where(seen, jnp.exp(res_scores - res_top), 0.0)
    res_total = jnp.sum(res_weights, axis=1, keepdims=True)
    res_part = jnp.dot(
        res_weights.astype(jnp.bfloat16), rv_v[...], preferred_element_type=jnp.float32
    )

    pltpu.make_async_copy(
        st_all.at[pl.ds(0, S - 1)], st_all.at[pl.ds(0, S - 1)], recv_sem.at[2]
    ).wait()
    pltpu.make_async_copy(
        o_all.at[pl.ds(0, S - 1)], o_all.at[pl.ds(0, S - 1)], recv_sem.at[1]
    ).wait()
    tops = jnp.concatenate([st_all[:, 0, :], jnp.full((128 - S, 128), FLOOR, jnp.float32)], axis=0)
    totals = jnp.concatenate([st_all[:, 1, :], jnp.zeros((128 - S, 128), jnp.float32)], axis=0)
    tr_v[0] = tops.T
    tr_v[1] = totals.T
    mine = pl.multiple_of(16 * lax.rem(me, 8), 16)
    tops = tr_v[0, pl.ds(mine, 16), :]
    totals = tr_v[1, pl.ds(mine, 16), :]
    highest = jnp.maximum(jnp.max(tops, axis=1, keepdims=True), res_top)
    factor = jnp.exp(tops - highest)
    res_factor = jnp.exp(res_top - highest)
    whole = jnp.sum(factor * totals, axis=1, keepdims=True) + res_factor * res_total
    attended = res_part * res_factor
    for i in range(S):
        attended = attended + factor[:, i : i + 1] * o_all[i].astype(jnp.float32)
    attended = attended / whole
    turned = [attended] + [pltpu.roll(attended, 4 * n, 0) for n in range(1, 4)]

    ow_copy.wait()
    group = lax.shift_right_logical(lax.broadcasted_iota(jnp.int32, (16, 512), 0), 2)
    placed = [
        jnp.where(
            group == c, jnp.concatenate([turned[(c - h) % 4] for h in range(4)], axis=1), 0.0
        ).astype(jnp.bfloat16)
        for c in range(4)
    ]
    for p in range(NP):
        share = sum(
            jnp.dot(
                placed[c],
                ow_v[:, COL4 * c + PC * p : COL4 * c + PC * (p + 1)],
                preferred_element_type=jnp.float32,
            )
            for c in range(4)
        ).astype(jnp.bfloat16)
        tp_send[p] = share
        for peer in tp_peers(mt):
            pltpu.make_async_remote_copy(
                src_ref=tp_send.at[p],
                dst_ref=tp_all.at[mt, p],
                send_sem=send_sem.at[3],
                recv_sem=recv_sem.at[3],
                device_id={"tp": peer},
                device_id_type=MESH,
            ).start()
        tp_all[mt, p] = share
    pltpu.make_async_copy(
        tp_all.at[pl.ds(0, T - 1)], tp_all.at[pl.ds(0, T - 1)], recv_sem.at[3]
    ).wait()
    for p in range(NP):
        mixed = sum(tp_all[t, p].astype(jnp.float32) for t in range(T))
        for c in range(4):
            out_ref[:, COL4 * c + PC * p : COL4 * c + PC * (p + 1)] = mixed[
                4 * c : 4 * c + 4, :
            ].astype(jnp.bfloat16)

    for sem, buffer, n in ((0, q_all, S), (1, o_all, S), (2, st_all, S), (3, tp_all, T)):
        part_ref = buffer.at[pl.ds(0, n - 1)]
        pltpu.make_async_copy(part_ref, part_ref, send_sem.at[sem]).wait()


def local(x, w, gain, q, rk, rv, pt, div, length, ow):
    bf16, f32, i32 = jnp.bfloat16, jnp.float32, jnp.int32
    hbm = pl.BlockSpec(memory_space=pl.ANY)
    V = pltpu.VMEM
    return pl.pallas_call(
        kernel,
        out_shape=jax.ShapeDtypeStruct((4, D), bf16),
        in_specs=[hbm] * 11,
        out_specs=pl.BlockSpec(memory_space=pltpu.VMEM),
        scratch_shapes=[
            V((ROWS, D), bf16),
            V((2 * D, HD), bf16),
            V((D, 256), bf16),
            V((1, HD), f32),
            V((4, 512), bf16),
            V((2048, HD), bf16),
            V((2048, HD), bf16),
            pltpu.SMEM((4, 4), i32),
            pltpu.SMEM((1, 128), i32),
            pltpu.SMEM((1, 128), i32),
            V((1, 128), i32),
            V((1, 128), i32),
            V((512, D), bf16),
            V((584, HD), f32),
            V((16, HD), bf16),
            V((16, HD), bf16),
            V((S, 16, HD), bf16),
            V((S, 16, HD), bf16),
            V((S, 16, HD), bf16),
            V((4, 2, 128), f32),
            V((S, 2, 128), f32),
            V((2, 128, 128), f32),
            V((NP, 16, PC), bf16),
            V((T, NP, 16, PC), bf16),
            pltpu.SemaphoreType.DMA((8,)),
            pltpu.SemaphoreType.DMA((2, NC)),
            pltpu.SemaphoreType.DMA((2,)),
            pltpu.SemaphoreType.DMA,
            pltpu.SemaphoreType.DMA((4,)),
            pltpu.SemaphoreType.DMA((4,)),
        ],
        compiler_params=pltpu.CompilerParams(
            collective_id=0, has_side_effects=True, vmem_limit_bytes=40 * 1024 * 1024
        ),
        cost_estimate=pl.CostEstimate(
            flops=1_500_000_000, bytes_accessed=12_000_000, transcendentals=200_000
        ),
    )(
        *(
            pltpu.with_memory_space_constraint(operand, pltpu.HBM)
            for operand in (
                x,
                w.reshape(2 * D, HD),
                gain.reshape(1, HD),
                q,
                rk.reshape(2048, HD),
                rv.reshape(2048, HD),
                pt,
                div.reshape(1, 128),
                length.reshape(1, 128),
                ow,
                jnp.asarray(rope_table()),
            )
        )
    )


def solution(mesh):
    return jax.shard_map(
        local,
        mesh=mesh,
        in_specs=(
            P("samp", None),
            P(None, None, "tp"),
            P(),
            P("samp", "tp"),
            P("samp", None, "tp"),
            P("samp", None, "tp"),
            P("samp", None),
            P(),
            P(),
            P("tp", None),
        ),
        out_specs=P("samp", None),
        check_vma=False,
    )
```

```python
import numpy as np
import jax
import jax.numpy as jnp
from jax import lax
from jax.experimental import pallas as pl
from jax.experimental.pallas import tpu as pltpu
from jax.sharding import PartitionSpec as P

ROPE_BASE = 1000000.0
NORM_EPS = 1e-06
FLOOR = -1e30
S = 32
T = 8
HD = 128
D = 5120
ROWS = 256
NC = 5
DC = D // NC
COL4 = D // 4
PC = 256
NP = COL4 // PC
MESH = pl.DeviceIdType.MESH

COS0, SIN0, COSB, SINB, FREQ = 0, 256, 512, 544, 576
STEPX, STEPZ, PLACE = 577, 581, 585

STEPS = sorted(
    ((dx, dz) for dx in range(4) for dz in range(8)),
    key=lambda step: (min(step[0], 4 - step[0]) + min(step[1], 8 - step[1]), step),
)
BACK = [STEPS.index((-dx % 4, -dz % 8)) for dx, dz in STEPS]
GROUPS, PER = 4, 8


def rope_table():
    freq = ROPE_BASE ** (-(np.arange(64, dtype=np.float64) * 2.0 / HD))
    freq = np.concatenate([freq, freq])
    row = np.arange(ROWS, dtype=np.float64)[:, None] * freq
    base = (np.arange(S, dtype=np.float64) * ROWS)[:, None] * freq
    last = np.zeros((16, HD))
    last[0] = freq
    for slot in range(S):
        lanes = slice(slot % PER * 16, slot % PER * 16 + 16)
        last[STEPX - FREQ + slot // PER, lanes] = STEPS[slot][0]
        last[STEPZ - FREQ + slot // PER, lanes] = STEPS[slot][1]
        last[PLACE - FREQ, slot] = BACK[slot] % PER
    return np.concatenate([np.cos(row), np.sin(row), np.cos(base), np.sin(base), last]).astype(
        np.float32
    )


def samp_peer(me, slot):
    dx, dz = STEPS[slot]
    x = jnp.bitwise_and(lax.shift_right_logical(me, 3) + dx, 3)
    return x * 8 + jnp.bitwise_and(me + dz, 7)


def tp_peers(mt):
    for dy in (2, 1, 3, 0):
        same = lax.rem(mt + 2 * dy, T)
        if dy:
            yield same
        yield same + 1 - 2 * lax.rem(same, 2)


def swap_halves(v):
    lane = lax.broadcasted_iota(jnp.int32, v.shape, 1)
    return jnp.where(lane < 64, -1.0, 1.0) * pltpu.roll(v, 64, 1)


def kernel(
    x_hbm,
    w_hbm,
    gain_hbm,
    q_hbm,
    rk_hbm,
    rv_hbm,
    pt_hbm,
    div_hbm,
    len_hbm,
    ow_hbm,
    tab_hbm,
    out_ref,
    x_v,
    w_v,
    wd,
    gain_v,
    q_v,
    rk_v,
    rv_v,
    pt_s,
    div_s,
    len_s,
    div_v,
    len_v,
    ow_v,
    tab_v,
    q_send,
    q_res,
    q_all,
    o_send,
    o_all,
    st_send,
    st_all,
    tr_v,
    tp_send,
    tp_all,
    small_sem,
    chunk_sem,
    page_sem,
    ow_sem,
    send_sem,
    recv_sem,
    q_sem,
):
    me = lax.axis_index("samp")
    mt = lax.axis_index("tp")

    barrier = pltpu.get_barrier_semaphore()
    for slot in range(S - 1, 0, -1):
        pl.semaphore_signal(
            barrier, inc=1, device_id={"samp": samp_peer(me, slot)}, device_id_type=MESH
        )
    for peer in tp_peers(mt):
        pl.semaphore_signal(barrier, inc=1, device_id={"tp": peer}, device_id_type=MESH)

    small = [
        pltpu.make_async_copy(src, dst, small_sem.at[i])
        for i, (src, dst) in enumerate(
            [
                (len_hbm, len_s),
                (div_hbm, div_s),
                (q_hbm, q_v),
                (tab_hbm, tab_v),
                (pt_hbm, pt_s),
                (len_hbm, len_v),
                (div_hbm, div_v),
                (gain_hbm, gain_v),
            ]
        )
    ]
    for copy in small:
        copy.start()
    w_copies = [
        pltpu.make_async_copy(
            w_hbm.at[pl.ds(c * 2 * DC, 2 * DC)], w_v.at[pl.ds(c * 2 * DC, 2 * DC)], chunk_sem.at[0, c]
        )
        for c in range(NC)
    ]
    x_copies = [
        pltpu.make_async_copy(
            x_hbm.at[:, pl.ds(c * DC, DC)], x_v.at[:, pl.ds(c * DC, DC)], chunk_sem.at[1, c]
        )
        for c in range(NC)
    ]
    for c in range(NC):
        w_copies[c].start()
        x_copies[c].start()
    pages = [
        pltpu.make_async_copy(rk_hbm, rk_v, page_sem.at[0]),
        pltpu.make_async_copy(rv_hbm, rv_v, page_sem.at[1]),
    ]
    for copy in pages:
        copy.start()
    ow_copy = pltpu.make_async_copy(ow_hbm, ow_v, ow_sem)
    ow_copy.start()

    for copy in small:
        copy.wait()
    row = lax.broadcasted_iota(jnp.int32, (16, HD), 0)
    sample = lax.rem(row, 4)

    def by_sample(values):
        return jnp.where(
            sample == 0,
            values[0],
            jnp.where(sample == 1, values[1], jnp.where(sample == 2, values[2], values[3])),
        )

    my_len = [len_s[0, me * 4 + i] for i in range(4)]
    my_div = [div_s[0, me * 4 + i] for i in range(4)]
    freq = tab_v[FREQ : FREQ + 1, :]
    q = q_v[...].astype(jnp.float32)
    q = jnp.concatenate([q[:, h * HD : (h + 1) * HD] for h in range(4)], axis=0)
    q_swapped = swap_halves(q)

    def rotate(positions):
        angle = by_sample(positions).astype(jnp.float32) * freq
        return (q * jnp.cos(angle) + q_swapped * jnp.sin(angle)).astype(jnp.bfloat16)

    q_app = rotate([my_len[i] - 128 * my_div[i] for i in range(4)])
    q_res[...] = rotate(my_len)
    q_send[...] = q_app
    q_all[0] = q_app

    pl.semaphore_wait(barrier, S - 1 + T - 1)

    for slot in range(S - 1, 0, -1):
        pltpu.make_async_remote_copy(
            src_ref=q_send,
            dst_ref=q_all.at[BACK[slot]],
            send_sem=send_sem.at[0],
            recv_sem=q_sem.at[BACK[slot] // PER],
            device_id={"samp": samp_peer(me, slot)},
            device_id_type=MESH,
        ).start()

    used = len_v[...] - 128 * div_v[...]
    high = lax.shift_right_logical(used, 7)
    low = used - 128 * high
    pair_row = lax.broadcasted_iota(jnp.int32, (16, 128), 0)
    pair = jnp.where(pair_row == 0, high, jnp.where(pair_row == 1, low, 0))
    pair = pair.astype(jnp.float32).astype(jnp.bfloat16)
    e_row = lax.broadcasted_iota(jnp.int32, (128, 128), 0)
    e_col = lax.broadcasted_iota(jnp.int32, (1, 128), 1)
    used_wide = []
    for g in range(GROUPS):
        step_x = tab_v[STEPX + g : STEPX + g + 1, :].astype(jnp.int32)
        step_z = tab_v[STEPZ + g : STEPZ + g + 1, :].astype(jnp.int32)
        owner = jnp.bitwise_and(step_x + lax.shift_right_logical(me, 3), 3) * 8
        owner = owner + jnp.bitwise_and(step_z + me, 7)
        spread = jnp.where(e_row == 4 * owner + jnp.bitwise_and(e_col, 3), 1.0, 0.0)
        wide = jnp.dot(pair, spread.astype(jnp.bfloat16), preferred_element_type=jnp.float32)
        used_wide.append((wide[0:1] * 128.0 + wide[1:2]).astype(jnp.int32))

    p_row = lax.broadcasted_iota(jnp.int32, (256, 256), 0)
    p_col = lax.broadcasted_iota(jnp.int32, (256, 256), 1)
    perm = jnp.where(
        p_col == jnp.where(p_row < 128, 2 * p_row, 2 * p_row - 255), 1.0, 0.0
    ).astype(jnp.bfloat16)
    acc = jnp.zeros((ROWS, 256), jnp.float32)
    for c in range(NC):
        w_copies[c].wait()
        for i in range(c * DC // 256, (c + 1) * DC // 256):
            pairs = jnp.concatenate(
                [w_v[pl.ds(i * 512, 256), :], w_v[pl.ds(i * 512 + 256, 256), :]], axis=1
            )
            apart = jnp.dot(perm, pairs, preferred_element_type=jnp.float32).astype(jnp.bfloat16)
            wd[pl.ds(i * 256, 128), 0:128] = apart[0:128, 0:128]
            wd[pl.ds(i * 256, 128), 128:256] = apart[128:256, 0:128]
            wd[pl.ds(i * 256 + 128, 128), 0:128] = apart[0:128, 128:256]
            wd[pl.ds(i * 256 + 128, 128), 128:256] = apart[128:256, 128:256]
        x_copies[c].wait()
        acc = acc + jnp.dot(
            x_v[:, c * DC : (c + 1) * DC],
            wd[c * DC : (c + 1) * DC, :],
            preferred_element_type=jnp.float32,
        )
    raw = acc[:, 0:128]
    values = acc[:, 128:256].astype(jnp.bfloat16)
    scale = lax.rsqrt(jnp.mean(raw * raw, axis=1, keepdims=True) + NORM_EPS)
    keys = raw * scale * gain_v[...]
    cos_b = tab_v[pl.ds(COSB + me, 1), :]
    sin_b = tab_v[pl.ds(SINB + me, 1), :]
    cos_0 = tab_v[COS0 : COS0 + ROWS, :]
    sin_0 = tab_v[SIN0 : SIN0 + ROWS, :]
    cos = cos_0 * cos_b - sin_0 * sin_b
    sin = sin_0 * cos_b + cos_0 * sin_b
    keys = (keys * cos + swap_halves(keys) * sin).astype(jnp.bfloat16)

    position = lax.broadcasted_iota(jnp.int32, (ROWS, PER * 16), 0) + me * ROWS
    for g in range(GROUPS):
        first = 1 if g == 0 else PER * g
        fresh = q_all.at[pl.ds(first, PER * (g + 1) - first)]
        pltpu.make_async_copy(fresh, fresh, q_sem.at[g]).wait()
        scores = lax.dot_general(
            keys,
            q_all[PER * g : PER * (g + 1)].reshape(PER * 16, HD),
            (((1,), (1,)), ((), ())),
            preferred_element_type=jnp.float32,
        ) * (HD**-0.5)
        valid = position < used_wide[g]
        top = jnp.max(jnp.where(valid, scores, FLOOR), axis=0, keepdims=True)
        weights = jnp.where(valid, jnp.exp(scores - top), 0.0)
        total = jnp.sum(weights, axis=0, keepdims=True)
        part = lax.dot_general(
            weights.astype(jnp.bfloat16),
            values,
            (((0,), (0,)), ((), ())),
            preferred_element_type=jnp.float32,
        ).astype(jnp.bfloat16)
        o_send[PER * g : PER * (g + 1)] = part.reshape(PER, 16, HD)
        st_send[g, 0:1, :] = top
        st_send[g, 1:2, :] = total
        for slot in range(PER * (g + 1) - 1, first - 1, -1):
            pltpu.make_async_remote_copy(
                src_ref=st_send.at[g],
                dst_ref=st_all.at[BACK[slot]],
                send_sem=send_sem.at[2],
                recv_sem=recv_sem.at[1],
                device_id={"samp": samp_peer(me, slot)},
                device_id_type=MESH,
            ).start()
            pltpu.make_async_remote_copy(
                src_ref=o_send.at[slot],
                dst_ref=o_all.at[BACK[slot]],
                send_sem=send_sem.at[1],
                recv_sem=recv_sem.at[0],
                device_id={"samp": samp_peer(me, slot)},
                device_id_type=MESH,
            ).start()
    o_all[0] = o_send[0]
    st_all[0] = st_send[0]

    for copy in pages:
        copy.wait()
    lane = lax.broadcasted_iota(jnp.int32, (16, HD), 1)
    slot_ok = jnp.zeros((16, HD), jnp.float32)
    for j in range(4):
        page = by_sample([pt_s[i, j] for i in range(4)])
        count = by_sample(my_div)
        slot_ok = jnp.where((lane == page) & (count > j), 1.0, slot_ok)
    seen = jnp.concatenate(
        [jnp.broadcast_to(slot_ok[:, k : k + 1], (16, HD)) for k in range(16)], axis=1
    ) > 0.5
    res_scores = lax.dot_general(
        q_res[...], rk_v[...], (((1,), (1,)), ((), ())), preferred_element_type=jnp.float32
    ) * (HD**-0.5)
    res_top = jnp.max(jnp.where(seen, res_scores, FLOOR), axis=1, keepdims=True)
    res_weights = jnp.where(seen, jnp.exp(res_scores - res_top), 0.0)
    res_total = jnp.sum(res_weights, axis=1, keepdims=True)
    res_part = jnp.dot(
        res_weights.astype(jnp.bfloat16), rv_v[...], preferred_element_type=jnp.float32
    )

    pltpu.make_async_copy(
        st_all.at[pl.ds(0, S - 1)], st_all.at[pl.ds(0, S - 1)], recv_sem.at[1]
    ).wait()
    pltpu.make_async_copy(
        o_all.at[pl.ds(0, S - 1)], o_all.at[pl.ds(0, S - 1)], recv_sem.at[0]
    ).wait()
    tops = jnp.concatenate([st_all[:, 0, :], jnp.full((128 - S, 128), FLOOR, jnp.float32)], axis=0)
    totals = jnp.concatenate([st_all[:, 1, :], jnp.zeros((128 - S, 128), jnp.float32)], axis=0)
    tr_v[0] = tops.T
    tr_v[1] = totals.T
    place = tab_v[PLACE : PLACE + 1, :]
    tops, totals = tr_v[0, 0:16, :], tr_v[1, 0:16, :]
    for n in range(1, PER):
        here = jnp.broadcast_to(place, (16, HD)) == float(n)
        tops = jnp.where(here, tr_v[0, 16 * n : 16 * n + 16, :], tops)
        totals = jnp.where(here, tr_v[1, 16 * n : 16 * n + 16, :], totals)
    highest = jnp.maximum(jnp.max(tops, axis=1, keepdims=True), res_top)
    factor = jnp.exp(tops - highest)
    res_factor = jnp.exp(res_top - highest)
    whole = jnp.sum(factor * totals, axis=1, keepdims=True) + res_factor * res_total
    attended = res_part * res_factor
    for i in range(S):
        attended = attended + factor[:, i : i + 1] * o_all[i].astype(jnp.float32)
    attended = attended / whole
    turned = [attended] + [pltpu.roll(attended, 4 * n, 0) for n in range(1, 4)]

    ow_copy.wait()
    group = lax.shift_right_logical(lax.broadcasted_iota(jnp.int32, (16, 512), 0), 2)
    placed = [
        jnp.where(
            group == c, jnp.concatenate([turned[(c - h) % 4] for h in range(4)], axis=1), 0.0
        ).astype(jnp.bfloat16)
        for c in range(4)
    ]
    for p in range(NP):
        share = sum(
            jnp.dot(
                placed[c],
                ow_v[:, COL4 * c + PC * p : COL4 * c + PC * (p + 1)],
                preferred_element_type=jnp.float32,
            )
            for c in range(4)
        ).astype(jnp.bfloat16)
        tp_send[p] = share
        for peer in tp_peers(mt):
            pltpu.make_async_remote_copy(
                src_ref=tp_send.at[p],
                dst_ref=tp_all.at[mt, p],
                send_sem=send_sem.at[3],
                recv_sem=recv_sem.at[2],
                device_id={"tp": peer},
                device_id_type=MESH,
            ).start()
        tp_all[mt, p] = share
    pltpu.make_async_copy(
        tp_all.at[pl.ds(0, T - 1)], tp_all.at[pl.ds(0, T - 1)], recv_sem.at[2]
    ).wait()
    for p in range(NP):
        mixed = sum(tp_all[t, p].astype(jnp.float32) for t in range(T))
        for c in range(4):
            out_ref[:, COL4 * c + PC * p : COL4 * c + PC * (p + 1)] = mixed[
                4 * c : 4 * c + 4, :
            ].astype(jnp.bfloat16)

    for sem, buffer, n in ((0, q_all, S), (1, o_all, S), (2, st_all, S), (3, tp_all, T)):
        part_ref = buffer.at[pl.ds(0, n - 1)]
        pltpu.make_async_copy(part_ref, part_ref, send_sem.at[sem]).wait()


def local(x, w, gain, q, rk, rv, pt, div, length, ow):
    bf16, f32, i32 = jnp.bfloat16, jnp.float32, jnp.int32
    hbm = pl.BlockSpec(memory_space=pl.ANY)
    V = pltpu.VMEM
    return pl.pallas_call(
        kernel,
        out_shape=jax.ShapeDtypeStruct((4, D), bf16),
        in_specs=[hbm] * 11,
        out_specs=pl.BlockSpec(memory_space=pltpu.VMEM),
        scratch_shapes=[
            V((ROWS, D), bf16),
            V((2 * D, HD), bf16),
            V((D, 256), bf16),
            V((1, HD), f32),
            V((4, 512), bf16),
            V((2048, HD), bf16),
            V((2048, HD), bf16),
            pltpu.SMEM((4, 4), i32),
            pltpu.SMEM((1, 128), i32),
            pltpu.SMEM((1, 128), i32),
            V((1, 128), i32),
            V((1, 128), i32),
            V((512, D), bf16),
            V((592, HD), f32),
            V((16, HD), bf16),
            V((16, HD), bf16),
            V((S, 16, HD), bf16),
            V((S, 16, HD), bf16),
            V((S, 16, HD), bf16),
            V((4, 2, 128), f32),
            V((S, 2, 128), f32),
            V((2, 128, 128), f32),
            V((NP, 16, PC), bf16),
            V((T, NP, 16, PC), bf16),
            pltpu.SemaphoreType.DMA((8,)),
            pltpu.SemaphoreType.DMA((2, NC)),
            pltpu.SemaphoreType.DMA((2,)),
            pltpu.SemaphoreType.DMA,
            pltpu.SemaphoreType.DMA((4,)),
            pltpu.SemaphoreType.DMA((3,)),
            pltpu.SemaphoreType.DMA((GROUPS,)),
        ],
        compiler_params=pltpu.CompilerParams(
            collective_id=0, has_side_effects=True, vmem_limit_bytes=40 * 1024 * 1024
        ),
        cost_estimate=pl.CostEstimate(
            flops=1_500_000_000, bytes_accessed=12_000_000, transcendentals=200_000
        ),
    )(
        *(
            pltpu.with_memory_space_constraint(operand, pltpu.HBM)
            for operand in (
                x,
                w.reshape(2 * D, HD),
                gain.reshape(1, HD),
                q,
                rk.reshape(2048, HD),
                rv.reshape(2048, HD),
                pt,
                div.reshape(1, 128),
                length.reshape(1, 128),
                ow,
                jnp.asarray(rope_table()),
            )
        )
    )


def solution(mesh):
    return jax.shard_map(
        local,
        mesh=mesh,
        in_specs=(
            P("samp", None),
            P(None, None, "tp"),
            P(),
            P("samp", "tp"),
            P("samp", None, "tp"),
            P("samp", None, "tp"),
            P("samp", None),
            P(),
            P(),
            P("tp", None),
        ),
        out_specs=P("samp", None),
        check_vma=False,
    )
```

```python
import numpy as np
import jax
import jax.numpy as jnp
from jax import lax
from jax.experimental import pallas as pl
from jax.experimental.pallas import tpu as pltpu
from jax.sharding import PartitionSpec as P

ROPE_BASE = 1000000.0
NORM_EPS = 1e-06
FLOOR = -1e30
S = 32
T = 8
HD = 128
D = 5120
ROWS = 256
NC = 5
DC = D // NC
COL4 = D // 4
PC = 256
NP = COL4 // PC
MESH = pl.DeviceIdType.MESH

COS0, SIN0, COSB, SINB, FREQ = 0, 256, 512, 544, 576
STEPX, STEPZ, PLACE = 577, 581, 585

STEPS = sorted(
    ((dx, dz) for dx in range(4) for dz in range(8)),
    key=lambda step: (min(step[0], 4 - step[0]) + min(step[1], 8 - step[1]), step),
)
BACK = [STEPS.index((-dx % 4, -dz % 8)) for dx, dz in STEPS]
GROUPS, PER = 4, 8


def rope_table():
    freq = ROPE_BASE ** (-(np.arange(64, dtype=np.float64) * 2.0 / HD))
    freq = np.concatenate([freq, freq])
    row = np.arange(ROWS, dtype=np.float64)[:, None] * freq
    base = (np.arange(S, dtype=np.float64) * ROWS)[:, None] * freq
    last = np.zeros((16, HD))
    last[0] = freq
    for slot in range(S):
        lanes = slice(slot % PER * 16, slot % PER * 16 + 16)
        last[STEPX - FREQ + slot // PER, lanes] = STEPS[slot][0]
        last[STEPZ - FREQ + slot // PER, lanes] = STEPS[slot][1]
        last[PLACE - FREQ, slot] = BACK[slot] % 4
    return np.concatenate([np.cos(row), np.sin(row), np.cos(base), np.sin(base), last]).astype(
        np.float32
    )


def samp_peer(me, slot):
    dx, dz = STEPS[slot]
    x = jnp.bitwise_and(lax.shift_right_logical(me, 3) + dx, 3)
    return x * 8 + jnp.bitwise_and(me + dz, 7)


def tp_peers(mt):
    for dy in (2, 1, 3, 0):
        same = lax.rem(mt + 2 * dy, T)
        if dy:
            yield same
        yield same + 1 - 2 * lax.rem(same, 2)


def swap_halves(v):
    lane = lax.broadcasted_iota(jnp.int32, v.shape, 1)
    return jnp.where(lane < 64, -1.0, 1.0) * pltpu.roll(v, 64, 1)


def kernel(
    x_hbm,
    w_hbm,
    gain_hbm,
    q_hbm,
    rk_hbm,
    rv_hbm,
    pt_hbm,
    div_hbm,
    len_hbm,
    ow_hbm,
    tab_hbm,
    out_ref,
    x_v,
    w_v,
    wd,
    gain_v,
    q_v,
    rk_v,
    rv_v,
    pt_s,
    div_s,
    len_s,
    div_v,
    len_v,
    ow_v,
    tab_v,
    q_send,
    q_res,
    q_all,
    o_send,
    o_all,
    st_send,
    st_all,
    tr_v,
    tp_send,
    tp_all,
    small_sem,
    chunk_sem,
    page_sem,
    ow_sem,
    send_sem,
    recv_sem,
    q_sem,
    tp_sem,
):
    me = lax.axis_index("samp")
    mt = lax.axis_index("tp")

    barrier = pltpu.get_barrier_semaphore()
    for slot in range(S - 1, 0, -1):
        pl.semaphore_signal(
            barrier, inc=1, device_id={"samp": samp_peer(me, slot)}, device_id_type=MESH
        )
    for peer in tp_peers(mt):
        pl.semaphore_signal(barrier, inc=1, device_id={"tp": peer}, device_id_type=MESH)

    small = [
        pltpu.make_async_copy(src, dst, small_sem.at[i])
        for i, (src, dst) in enumerate(
            [
                (len_hbm, len_s),
                (div_hbm, div_s),
                (q_hbm, q_v),
                (tab_hbm, tab_v),
                (pt_hbm, pt_s),
                (len_hbm, len_v),
                (div_hbm, div_v),
                (gain_hbm, gain_v),
            ]
        )
    ]
    for copy in small:
        copy.start()
    w_copies = [
        pltpu.make_async_copy(
            w_hbm.at[pl.ds(c * 2 * DC, 2 * DC)], w_v.at[pl.ds(c * 2 * DC, 2 * DC)], chunk_sem.at[0, c]
        )
        for c in range(NC)
    ]
    x_copies = [
        pltpu.make_async_copy(
            x_hbm.at[:, pl.ds(c * DC, DC)], x_v.at[:, pl.ds(c * DC, DC)], chunk_sem.at[1, c]
        )
        for c in range(NC)
    ]
    for copy in w_copies + x_copies:
        copy.start()
    pages = [
        pltpu.make_async_copy(rk_hbm, rk_v, page_sem.at[0]),
        pltpu.make_async_copy(rv_hbm, rv_v, page_sem.at[1]),
    ]
    for copy in pages:
        copy.start()
    ow_copy = pltpu.make_async_copy(ow_hbm, ow_v, ow_sem)
    ow_copy.start()

    for copy in small:
        copy.wait()
    row = lax.broadcasted_iota(jnp.int32, (16, HD), 0)
    sample = lax.rem(row, 4)

    def by_sample(values):
        return jnp.where(
            sample == 0,
            values[0],
            jnp.where(sample == 1, values[1], jnp.where(sample == 2, values[2], values[3])),
        )

    my_len = [len_s[0, me * 4 + i] for i in range(4)]
    my_div = [div_s[0, me * 4 + i] for i in range(4)]
    freq = tab_v[FREQ : FREQ + 1, :]
    q = q_v[...].astype(jnp.float32)
    q = jnp.concatenate([q[:, h * HD : (h + 1) * HD] for h in range(4)], axis=0)
    q_swapped = swap_halves(q)

    def rotate(positions):
        angle = by_sample(positions).astype(jnp.float32) * freq
        return (q * jnp.cos(angle) + q_swapped * jnp.sin(angle)).astype(jnp.bfloat16)

    q_app = rotate([my_len[i] - 128 * my_div[i] for i in range(4)])
    q_res[...] = rotate(my_len)
    q_send[...] = q_app
    q_all[0] = q_app

    used = len_v[...] - 128 * div_v[...]
    high = lax.shift_right_logical(used, 7)
    low = used - 128 * high
    pair_row = lax.broadcasted_iota(jnp.int32, (16, 128), 0)
    pair = jnp.where(pair_row == 0, high, jnp.where(pair_row == 1, low, 0))
    pair = pair.astype(jnp.float32).astype(jnp.bfloat16)
    e_row = lax.broadcasted_iota(jnp.int32, (128, 128), 0)
    e_col = lax.broadcasted_iota(jnp.int32, (1, 128), 1)
    used_wide = []
    for g in range(GROUPS):
        step_x = tab_v[STEPX + g : STEPX + g + 1, :].astype(jnp.int32)
        step_z = tab_v[STEPZ + g : STEPZ + g + 1, :].astype(jnp.int32)
        owner = jnp.bitwise_and(step_x + lax.shift_right_logical(me, 3), 3) * 8
        owner = owner + jnp.bitwise_and(step_z + me, 7)
        spread = jnp.where(e_row == 4 * owner + jnp.bitwise_and(e_col, 3), 1.0, 0.0)
        wide = jnp.dot(pair, spread.astype(jnp.bfloat16), preferred_element_type=jnp.float32)
        used_wide.append((wide[0:1] * 128.0 + wide[1:2]).astype(jnp.int32))

    p_row = lax.broadcasted_iota(jnp.int32, (256, 256), 0)
    p_col = lax.broadcasted_iota(jnp.int32, (256, 256), 1)
    perm = jnp.where(
        p_col == jnp.where(p_row < 128, 2 * p_row, 2 * p_row - 255), 1.0, 0.0
    ).astype(jnp.bfloat16)
    for c in range(NC):
        w_copies[c].wait()
        for i in range(c * DC // 256, (c + 1) * DC // 256):
            pairs = jnp.concatenate(
                [w_v[pl.ds(i * 512, 256), :], w_v[pl.ds(i * 512 + 256, 256), :]], axis=1
            )
            apart = jnp.dot(perm, pairs, preferred_element_type=jnp.float32).astype(jnp.bfloat16)
            wd[pl.ds(i * 256, 128), 0:128] = apart[0:128, 0:128]
            wd[pl.ds(i * 256, 128), 128:256] = apart[128:256, 0:128]
            wd[pl.ds(i * 256 + 128, 128), 0:128] = apart[0:128, 128:256]
            wd[pl.ds(i * 256 + 128, 128), 128:256] = apart[128:256, 128:256]

    pl.semaphore_wait(barrier, S - 1 + T - 1)

    for slot in range(S - 1, 0, -1):
        pltpu.make_async_remote_copy(
            src_ref=q_send,
            dst_ref=q_all.at[BACK[slot]],
            send_sem=send_sem.at[0],
            recv_sem=q_sem.at[BACK[slot] // PER],
            device_id={"samp": samp_peer(me, slot)},
            device_id_type=MESH,
        ).start()

    acc = jnp.zeros((ROWS, 256), jnp.float32)
    for c in range(NC):
        x_copies[c].wait()
        acc = acc + jnp.dot(
            x_v[:, c * DC : (c + 1) * DC],
            wd[c * DC : (c + 1) * DC, :],
            preferred_element_type=jnp.float32,
        )
    raw = acc[:, 0:128]
    values = acc[:, 128:256].astype(jnp.bfloat16)
    scale = lax.rsqrt(jnp.mean(raw * raw, axis=1, keepdims=True) + NORM_EPS)
    keys = raw * scale * gain_v[...]
    cos_b = tab_v[pl.ds(COSB + me, 1), :]
    sin_b = tab_v[pl.ds(SINB + me, 1), :]
    cos_0 = tab_v[COS0 : COS0 + ROWS, :]
    sin_0 = tab_v[SIN0 : SIN0 + ROWS, :]
    cos = cos_0 * cos_b - sin_0 * sin_b
    sin = sin_0 * cos_b + cos_0 * sin_b
    keys = (keys * cos + swap_halves(keys) * sin).astype(jnp.bfloat16)

    position = lax.broadcasted_iota(jnp.int32, (ROWS, PER * 16), 0) + me * ROWS
    for g in reversed(range(GROUPS)):
        first = 1 if g == 0 else PER * g
        fresh = q_all.at[pl.ds(first, PER * (g + 1) - first)]
        pltpu.make_async_copy(fresh, fresh, q_sem.at[g]).wait()
        scores = lax.dot_general(
            keys,
            q_all[PER * g : PER * (g + 1)].reshape(PER * 16, HD),
            (((1,), (1,)), ((), ())),
            preferred_element_type=jnp.float32,
        ) * (HD**-0.5)
        valid = position < used_wide[g]
        top = jnp.max(jnp.where(valid, scores, FLOOR), axis=0, keepdims=True)
        weights = jnp.where(valid, jnp.exp(scores - top), 0.0)
        total = jnp.sum(weights, axis=0, keepdims=True)
        part = lax.dot_general(
            weights.astype(jnp.bfloat16),
            values,
            (((0,), (0,)), ((), ())),
            preferred_element_type=jnp.float32,
        ).astype(jnp.bfloat16)
        o_send[PER * g : PER * (g + 1)] = part.reshape(PER, 16, HD)
        for half in (0, 1):
            lanes = slice(64 * half, 64 * half + 64)
            st_send[2 * g + half] = jnp.concatenate([top[:, lanes], total[:, lanes]], axis=1)
        for slot in range(PER * (g + 1) - 1, first - 1, -1):
            pltpu.make_async_remote_copy(
                src_ref=st_send.at[slot // 4],
                dst_ref=st_all.at[BACK[slot]],
                send_sem=send_sem.at[2],
                recv_sem=recv_sem.at[1],
                device_id={"samp": samp_peer(me, slot)},
                device_id_type=MESH,
            ).start()
            pltpu.make_async_remote_copy(
                src_ref=o_send.at[slot],
                dst_ref=o_all.at[BACK[slot]],
                send_sem=send_sem.at[1],
                recv_sem=recv_sem.at[0],
                device_id={"samp": samp_peer(me, slot)},
                device_id_type=MESH,
            ).start()
    o_all[0] = o_send[0]
    st_all[0] = st_send[0]

    for copy in pages:
        copy.wait()
    lane = lax.broadcasted_iota(jnp.int32, (16, HD), 1)
    slot_ok = jnp.zeros((16, HD), jnp.float32)
    for j in range(4):
        page = by_sample([pt_s[i, j] for i in range(4)])
        count = by_sample(my_div)
        slot_ok = jnp.where((lane == page) & (count > j), 1.0, slot_ok)
    seen = jnp.concatenate(
        [jnp.broadcast_to(slot_ok[:, k : k + 1], (16, HD)) for k in range(16)], axis=1
    ) > 0.5
    res_scores = lax.dot_general(
        q_res[...], rk_v[...], (((1,), (1,)), ((), ())), preferred_element_type=jnp.float32
    ) * (HD**-0.5)
    res_top = jnp.max(jnp.where(seen, res_scores, FLOOR), axis=1, keepdims=True)
    res_weights = jnp.where(seen, jnp.exp(res_scores - res_top), 0.0)
    res_total = jnp.sum(res_weights, axis=1, keepdims=True)
    res_part = jnp.dot(
        res_weights.astype(jnp.bfloat16), rv_v[...], preferred_element_type=jnp.float32
    )

    pltpu.make_async_copy(
        st_all.at[pl.ds(0, S - 1)], st_all.at[pl.ds(0, S - 1)], recv_sem.at[1]
    ).wait()
    tr_v[...] = jnp.concatenate(
        [st_all[:, 0, :], jnp.zeros((128 - S, 128), jnp.float32)], axis=0
    ).T
    place = jnp.broadcast_to(tab_v[PLACE : PLACE + 1, :], (16, HD))
    tops, totals = tr_v[0:16, :], tr_v[64:80, :]
    for n in range(1, 4):
        tops = jnp.where(place == float(n), tr_v[16 * n : 16 * n + 16, :], tops)
        totals = jnp.where(place == float(n), tr_v[16 * n + 64 : 16 * n + 80, :], totals)
    tops = jnp.where(lane < S, tops, FLOOR)
    highest = jnp.maximum(jnp.max(tops, axis=1, keepdims=True), res_top)
    factor = jnp.exp(tops - highest)
    res_factor = jnp.exp(res_top - highest)
    whole = jnp.sum(factor * totals, axis=1, keepdims=True) + res_factor * res_total
    pltpu.make_async_copy(
        o_all.at[pl.ds(0, S - 1)], o_all.at[pl.ds(0, S - 1)], recv_sem.at[0]
    ).wait()
    attended = [res_part * res_factor] + [jnp.zeros((16, HD), jnp.float32)] * 3
    for i in range(S):
        attended[i % 4] = attended[i % 4] + factor[:, i : i + 1] * o_all[i].astype(jnp.float32)
    attended = (attended[0] + attended[1] + attended[2] + attended[3]) / whole
    turned = [attended] + [pltpu.roll(attended, 4 * n, 0) for n in range(1, 4)]

    ow_copy.wait()
    group = lax.shift_right_logical(lax.broadcasted_iota(jnp.int32, (16, 512), 0), 2)
    placed = [
        jnp.where(
            group == c, jnp.concatenate([turned[(c - h) % 4] for h in range(4)], axis=1), 0.0
        ).astype(jnp.bfloat16)
        for c in range(4)
    ]
    for p in range(NP):
        share = sum(
            jnp.dot(
                placed[c],
                ow_v[:, COL4 * c + PC * p : COL4 * c + PC * (p + 1)],
                preferred_element_type=jnp.float32,
            )
            for c in range(4)
        ).astype(jnp.bfloat16)
        tp_send[p] = share
        for peer in tp_peers(mt):
            pltpu.make_async_remote_copy(
                src_ref=tp_send.at[p],
                dst_ref=tp_all.at[p, mt],
                send_sem=send_sem.at[3],
                recv_sem=tp_sem.at[p],
                device_id={"tp": peer},
                device_id_type=MESH,
            ).start()
        tp_all[p, mt] = share
    for p in range(NP):
        fresh = tp_all.at[p, pl.ds(0, T - 1)]
        pltpu.make_async_copy(fresh, fresh, tp_sem.at[p]).wait()
        mixed = sum(tp_all[p, t].astype(jnp.float32) for t in range(T))
        for c in range(4):
            out_ref[:, COL4 * c + PC * p : COL4 * c + PC * (p + 1)] = mixed[
                4 * c : 4 * c + 4, :
            ].astype(jnp.bfloat16)

    for sem, part_ref in (
        (0, q_all.at[pl.ds(0, S - 1)]),
        (1, o_all.at[pl.ds(0, S - 1)]),
        (2, st_all.at[pl.ds(0, S - 1)]),
        (3, tp_all.at[:, pl.ds(0, T - 1)]),
    ):
        pltpu.make_async_copy(part_ref, part_ref, send_sem.at[sem]).wait()


def local(x, w, gain, q, rk, rv, pt, div, length, ow):
    bf16, f32, i32 = jnp.bfloat16, jnp.float32, jnp.int32
    hbm = pl.BlockSpec(memory_space=pl.ANY)
    V = pltpu.VMEM
    return pl.pallas_call(
        kernel,
        out_shape=jax.ShapeDtypeStruct((4, D), bf16),
        in_specs=[hbm] * 11,
        out_specs=pl.BlockSpec(memory_space=pltpu.VMEM),
        scratch_shapes=[
            V((ROWS, D), bf16),
            V((2 * D, HD), bf16),
            V((D, 256), bf16),
            V((1, HD), f32),
            V((4, 512), bf16),
            V((2048, HD), bf16),
            V((2048, HD), bf16),
            pltpu.SMEM((4, 4), i32),
            pltpu.SMEM((1, 128), i32),
            pltpu.SMEM((1, 128), i32),
            V((1, 128), i32),
            V((1, 128), i32),
            V((512, D), bf16),
            V((592, HD), f32),
            V((16, HD), bf16),
            V((16, HD), bf16),
            V((S, 16, HD), bf16),
            V((S, 16, HD), bf16),
            V((S, 16, HD), bf16),
            V((2 * GROUPS, 1, 128), f32),
            V((S, 1, 128), f32),
            V((128, 128), f32),
            V((NP, 16, PC), bf16),
            V((NP, T, 16, PC), bf16),
            pltpu.SemaphoreType.DMA((8,)),
            pltpu.SemaphoreType.DMA((2, NC)),
            pltpu.SemaphoreType.DMA((2,)),
            pltpu.SemaphoreType.DMA,
            pltpu.SemaphoreType.DMA((4,)),
            pltpu.SemaphoreType.DMA((2,)),
            pltpu.SemaphoreType.DMA((GROUPS,)),
            pltpu.SemaphoreType.DMA((NP,)),
        ],
        compiler_params=pltpu.CompilerParams(
            collective_id=0, has_side_effects=True, vmem_limit_bytes=40 * 1024 * 1024
        ),
        cost_estimate=pl.CostEstimate(
            flops=1_500_000_000, bytes_accessed=12_000_000, transcendentals=200_000
        ),
    )(
        *(
            pltpu.with_memory_space_constraint(operand, pltpu.HBM)
            for operand in (
                x,
                w.reshape(2 * D, HD),
                gain.reshape(1, HD),
                q,
                rk.reshape(2048, HD),
                rv.reshape(2048, HD),
                pt,
                div.reshape(1, 128),
                length.reshape(1, 128),
                ow,
                jnp.asarray(rope_table()),
            )
        )
    )


def solution(mesh):
    return jax.shard_map(
        local,
        mesh=mesh,
        in_specs=(
            P("samp", None),
            P(None, None, "tp"),
            P(),
            P("samp", "tp"),
            P("samp", None, "tp"),
            P("samp", None, "tp"),
            P("samp", None),
            P(),
            P(),
            P("tp", None),
        ),
        out_specs=P("samp", None),
        check_vma=False,
    )
```

```python
import numpy as np
import jax
import jax.numpy as jnp
from jax import lax
from jax.experimental import pallas as pl
from jax.experimental.pallas import tpu as pltpu
from jax.sharding import PartitionSpec as P

ROPE_BASE = 1000000.0
NORM_EPS = 1e-06
FLOOR = -1e30
S = 32
T = 8
HD = 128
D = 5120
ROWS = 256
NC = 5
DC = D // NC
COL4 = D // 4
PC = 640
NP = COL4 // PC
MESH = pl.DeviceIdType.MESH

COS0, SIN0, COSB, SINB, FREQ = 0, 256, 512, 544, 576
STEPX, STEPZ, PLACE = 577, 581, 585

STEPS = sorted(
    ((dx, dz) for dx in range(4) for dz in range(8)),
    key=lambda step: (min(step[0], 4 - step[0]) + min(step[1], 8 - step[1]), step),
)
BACK = [STEPS.index((-dx % 4, -dz % 8)) for dx, dz in STEPS]
GROUPS, PER = 4, 8


def rope_table():
    freq = ROPE_BASE ** (-(np.arange(64, dtype=np.float64) * 2.0 / HD))
    freq = np.concatenate([freq, freq])
    row = np.arange(ROWS, dtype=np.float64)[:, None] * freq
    base = (np.arange(S, dtype=np.float64) * ROWS)[:, None] * freq
    last = np.zeros((16, HD))
    last[0] = freq
    for slot in range(S):
        lanes = slice(slot % PER * 16, slot % PER * 16 + 16)
        last[STEPX - FREQ + slot // PER, lanes] = STEPS[slot][0]
        last[STEPZ - FREQ + slot // PER, lanes] = STEPS[slot][1]
        last[PLACE - FREQ, slot] = BACK[slot] % 4
    return np.concatenate([np.cos(row), np.sin(row), np.cos(base), np.sin(base), last]).astype(
        np.float32
    )


def samp_peer(me, slot):
    dx, dz = STEPS[slot]
    x = jnp.bitwise_and(lax.shift_right_logical(me, 3) + dx, 3)
    return x * 8 + jnp.bitwise_and(me + dz, 7)


def tp_peers(mt):
    for dy in (2, 1, 3, 0):
        same = lax.rem(mt + 2 * dy, T)
        if dy:
            yield same
        yield same + 1 - 2 * lax.rem(same, 2)


def swap_halves(v):
    lane = lax.broadcasted_iota(jnp.int32, v.shape, 1)
    return jnp.where(lane < 64, -1.0, 1.0) * pltpu.roll(v, 64, 1)


def kernel(
    x_hbm,
    w_hbm,
    gain_hbm,
    q_hbm,
    rk_hbm,
    rv_hbm,
    pt_hbm,
    div_hbm,
    len_hbm,
    ow_hbm,
    tab_hbm,
    out_ref,
    x_v,
    w_v,
    wd,
    gain_v,
    q_v,
    rk_v,
    rv_v,
    pt_s,
    div_s,
    len_s,
    div_v,
    len_v,
    ow_v,
    tab_v,
    q_send,
    q_res,
    q_all,
    o_send,
    o_all,
    st_send,
    st_all,
    tr_v,
    tp_send,
    tp_all,
    small_sem,
    chunk_sem,
    page_sem,
    ow_sem,
    send_sem,
    recv_sem,
    q_sem,
    tp_sem,
):
    me = lax.axis_index("samp")
    mt = lax.axis_index("tp")

    barrier = pltpu.get_barrier_semaphore()
    for slot in range(S - 1, 0, -1):
        pl.semaphore_signal(
            barrier, inc=1, device_id={"samp": samp_peer(me, slot)}, device_id_type=MESH
        )
    for peer in tp_peers(mt):
        pl.semaphore_signal(barrier, inc=1, device_id={"tp": peer}, device_id_type=MESH)

    small = [
        pltpu.make_async_copy(src, dst, small_sem.at[i])
        for i, (src, dst) in enumerate(
            [
                (len_hbm, len_s),
                (div_hbm, div_s),
                (q_hbm, q_v),
                (tab_hbm, tab_v),
                (pt_hbm, pt_s),
                (len_hbm, len_v),
                (div_hbm, div_v),
                (gain_hbm, gain_v),
            ]
        )
    ]
    for copy in small:
        copy.start()
    w_copies = [
        pltpu.make_async_copy(
            w_hbm.at[pl.ds(c * 2 * DC, 2 * DC)], w_v.at[pl.ds(c * 2 * DC, 2 * DC)], chunk_sem.at[0, c]
        )
        for c in range(NC)
    ]
    x_copies = [
        pltpu.make_async_copy(
            x_hbm.at[:, pl.ds(c * DC, DC)], x_v.at[:, pl.ds(c * DC, DC)], chunk_sem.at[1, c]
        )
        for c in range(NC)
    ]
    for copy in w_copies + x_copies:
        copy.start()
    pages = [
        pltpu.make_async_copy(rk_hbm, rk_v, page_sem.at[0]),
        pltpu.make_async_copy(rv_hbm, rv_v, page_sem.at[1]),
    ]
    for copy in pages:
        copy.start()
    ow_copy = pltpu.make_async_copy(ow_hbm, ow_v, ow_sem)
    ow_copy.start()

    for copy in small:
        copy.wait()
    row = lax.broadcasted_iota(jnp.int32, (16, HD), 0)
    sample = lax.rem(row, 4)

    def by_sample(values):
        return jnp.where(
            sample == 0,
            values[0],
            jnp.where(sample == 1, values[1], jnp.where(sample == 2, values[2], values[3])),
        )

    my_len = [len_s[0, me * 4 + i] for i in range(4)]
    my_div = [div_s[0, me * 4 + i] for i in range(4)]
    freq = tab_v[FREQ : FREQ + 1, :]
    q = q_v[...].astype(jnp.float32)
    q = jnp.concatenate([q[:, h * HD : (h + 1) * HD] for h in range(4)], axis=0)
    q_swapped = swap_halves(q)

    def rotate(positions):
        angle = by_sample(positions).astype(jnp.float32) * freq
        return (q * jnp.cos(angle) + q_swapped * jnp.sin(angle)).astype(jnp.bfloat16)

    q_app = rotate([my_len[i] - 128 * my_div[i] for i in range(4)])
    q_res[...] = rotate(my_len)
    q_send[...] = q_app
    q_all[0] = q_app

    pl.semaphore_wait(barrier, S - 1 + T - 1)

    for slot in range(S - 1, 0, -1):
        pltpu.make_async_remote_copy(
            src_ref=q_send,
            dst_ref=q_all.at[BACK[slot]],
            send_sem=send_sem.at[0],
            recv_sem=q_sem.at[BACK[slot] // PER],
            device_id={"samp": samp_peer(me, slot)},
            device_id_type=MESH,
        ).start()

    used = len_v[...] - 128 * div_v[...]
    high = lax.shift_right_logical(used, 7)
    low = used - 128 * high
    pair_row = lax.broadcasted_iota(jnp.int32, (16, 128), 0)
    pair = jnp.where(pair_row == 0, high, jnp.where(pair_row == 1, low, 0))
    pair = pair.astype(jnp.float32).astype(jnp.bfloat16)
    e_row = lax.broadcasted_iota(jnp.int32, (128, 128), 0)
    e_col = lax.broadcasted_iota(jnp.int32, (1, 128), 1)
    used_wide = []
    for g in range(GROUPS):
        step_x = tab_v[STEPX + g : STEPX + g + 1, :].astype(jnp.int32)
        step_z = tab_v[STEPZ + g : STEPZ + g + 1, :].astype(jnp.int32)
        owner = jnp.bitwise_and(step_x + lax.shift_right_logical(me, 3), 3) * 8
        owner = owner + jnp.bitwise_and(step_z + me, 7)
        spread = jnp.where(e_row == 4 * owner + jnp.bitwise_and(e_col, 3), 1.0, 0.0)
        wide = jnp.dot(pair, spread.astype(jnp.bfloat16), preferred_element_type=jnp.float32)
        used_wide.append((wide[0:1] * 128.0 + wide[1:2]).astype(jnp.int32))

    p_row = lax.broadcasted_iota(jnp.int32, (256, 256), 0)
    p_col = lax.broadcasted_iota(jnp.int32, (256, 256), 1)
    perm = jnp.where(
        p_col == jnp.where(p_row < 128, 2 * p_row, 2 * p_row - 255), 1.0, 0.0
    ).astype(jnp.bfloat16)
    for c in range(NC):
        w_copies[c].wait()
        for i in range(c * DC // 256, (c + 1) * DC // 256):
            pairs = jnp.concatenate(
                [w_v[pl.ds(i * 512, 256), :], w_v[pl.ds(i * 512 + 256, 256), :]], axis=1
            )
            apart = jnp.dot(perm, pairs, preferred_element_type=jnp.float32).astype(jnp.bfloat16)
            wd[pl.ds(i * 256, 128), 0:128] = apart[0:128, 0:128]
            wd[pl.ds(i * 256, 128), 128:256] = apart[128:256, 0:128]
            wd[pl.ds(i * 256 + 128, 128), 0:128] = apart[0:128, 128:256]
            wd[pl.ds(i * 256 + 128, 128), 128:256] = apart[128:256, 128:256]

    acc = jnp.zeros((ROWS, 256), jnp.float32)
    for c in range(NC):
        x_copies[c].wait()
        acc = acc + jnp.dot(
            x_v[:, c * DC : (c + 1) * DC],
            wd[c * DC : (c + 1) * DC, :],
            preferred_element_type=jnp.float32,
        )
    raw = acc[:, 0:128]
    values = acc[:, 128:256].astype(jnp.bfloat16)
    scale = lax.rsqrt(jnp.mean(raw * raw, axis=1, keepdims=True) + NORM_EPS)
    keys = raw * scale * gain_v[...]
    cos_b = tab_v[pl.ds(COSB + me, 1), :]
    sin_b = tab_v[pl.ds(SINB + me, 1), :]
    cos_0 = tab_v[COS0 : COS0 + ROWS, :]
    sin_0 = tab_v[SIN0 : SIN0 + ROWS, :]
    cos = cos_0 * cos_b - sin_0 * sin_b
    sin = sin_0 * cos_b + cos_0 * sin_b
    keys = (keys * cos + swap_halves(keys) * sin).astype(jnp.bfloat16)

    position = lax.broadcasted_iota(jnp.int32, (ROWS, PER * 16), 0) + me * ROWS
    for g in reversed(range(GROUPS)):
        first = 1 if g == 0 else PER * g
        fresh = q_all.at[pl.ds(first, PER * (g + 1) - first)]
        pltpu.make_async_copy(fresh, fresh, q_sem.at[g]).wait()
        scores = lax.dot_general(
            keys,
            q_all[PER * g : PER * (g + 1)].reshape(PER * 16, HD),
            (((1,), (1,)), ((), ())),
            preferred_element_type=jnp.float32,
        ) * (HD**-0.5)
        valid = position < used_wide[g]
        top = jnp.max(jnp.where(valid, scores, FLOOR), axis=0, keepdims=True)
        weights = jnp.where(valid, jnp.exp(scores - top), 0.0)
        total = jnp.sum(weights, axis=0, keepdims=True)
        part = lax.dot_general(
            weights.astype(jnp.bfloat16),
            values,
            (((0,), (0,)), ((), ())),
            preferred_element_type=jnp.float32,
        ).astype(jnp.bfloat16)
        o_send[PER * g : PER * (g + 1)] = part.reshape(PER, 16, HD)
        for half in (0, 1):
            lanes = slice(64 * half, 64 * half + 64)
            st_send[2 * g + half] = jnp.concatenate([top[:, lanes], total[:, lanes]], axis=1)
        for slot in range(PER * (g + 1) - 1, first - 1, -1):
            pltpu.make_async_remote_copy(
                src_ref=st_send.at[slot // 4],
                dst_ref=st_all.at[BACK[slot]],
                send_sem=send_sem.at[2],
                recv_sem=recv_sem.at[1],
                device_id={"samp": samp_peer(me, slot)},
                device_id_type=MESH,
            ).start()
            pltpu.make_async_remote_copy(
                src_ref=o_send.at[slot],
                dst_ref=o_all.at[BACK[slot]],
                send_sem=send_sem.at[1],
                recv_sem=recv_sem.at[0],
                device_id={"samp": samp_peer(me, slot)},
                device_id_type=MESH,
            ).start()
    o_all[0] = o_send[0]
    st_all[0] = st_send[0]

    for copy in pages:
        copy.wait()
    lane = lax.broadcasted_iota(jnp.int32, (16, HD), 1)
    slot_ok = jnp.zeros((16, HD), jnp.float32)
    for j in range(4):
        page = by_sample([pt_s[i, j] for i in range(4)])
        count = by_sample(my_div)
        slot_ok = jnp.where((lane == page) & (count > j), 1.0, slot_ok)
    seen = jnp.concatenate(
        [jnp.broadcast_to(slot_ok[:, k : k + 1], (16, HD)) for k in range(16)], axis=1
    ) > 0.5
    res_scores = lax.dot_general(
        q_res[...], rk_v[...], (((1,), (1,)), ((), ())), preferred_element_type=jnp.float32
    ) * (HD**-0.5)
    res_top = jnp.max(jnp.where(seen, res_scores, FLOOR), axis=1, keepdims=True)
    res_weights = jnp.where(seen, jnp.exp(res_scores - res_top), 0.0)
    res_total = jnp.sum(res_weights, axis=1, keepdims=True)
    res_part = jnp.dot(
        res_weights.astype(jnp.bfloat16), rv_v[...], preferred_element_type=jnp.float32
    )

    pltpu.make_async_copy(
        st_all.at[pl.ds(0, S - 1)], st_all.at[pl.ds(0, S - 1)], recv_sem.at[1]
    ).wait()
    tr_v[...] = jnp.concatenate(
        [st_all[:, 0, :], jnp.zeros((128 - S, 128), jnp.float32)], axis=0
    ).T
    place = jnp.broadcast_to(tab_v[PLACE : PLACE + 1, :], (16, HD))
    tops, totals = tr_v[0:16, :], tr_v[64:80, :]
    for n in range(1, 4):
        tops = jnp.where(place == float(n), tr_v[16 * n : 16 * n + 16, :], tops)
        totals = jnp.where(place == float(n), tr_v[16 * n + 64 : 16 * n + 80, :], totals)
    tops = jnp.where(lane < S, tops, FLOOR)
    highest = jnp.maximum(jnp.max(tops, axis=1, keepdims=True), res_top)
    factor = jnp.exp(tops - highest)
    res_factor = jnp.exp(res_top - highest)
    whole = jnp.sum(factor * totals, axis=1, keepdims=True) + res_factor * res_total
    pltpu.make_async_copy(
        o_all.at[pl.ds(0, S - 1)], o_all.at[pl.ds(0, S - 1)], recv_sem.at[0]
    ).wait()
    attended = [res_part * res_factor] + [jnp.zeros((16, HD), jnp.float32)] * 3
    for i in range(S):
        attended[i % 4] = attended[i % 4] + factor[:, i : i + 1] * o_all[i].astype(jnp.float32)
    attended = (attended[0] + attended[1] + attended[2] + attended[3]) / whole
    turned = [attended] + [pltpu.roll(attended, 4 * n, 0) for n in range(1, 4)]

    ow_copy.wait()
    group = lax.shift_right_logical(lax.broadcasted_iota(jnp.int32, (16, 512), 0), 2)
    placed = [
        jnp.where(
            group == c, jnp.concatenate([turned[(c - h) % 4] for h in range(4)], axis=1), 0.0
        ).astype(jnp.bfloat16)
        for c in range(4)
    ]
    for p in range(NP):
        share = sum(
            jnp.dot(
                placed[c],
                ow_v[:, COL4 * c + PC * p : COL4 * c + PC * (p + 1)],
                preferred_element_type=jnp.float32,
            )
            for c in range(4)
        ).astype(jnp.bfloat16)
        tp_send[p] = share
        for peer in tp_peers(mt):
            pltpu.make_async_remote_copy(
                src_ref=tp_send.at[p],
                dst_ref=tp_all.at[p, mt],
                send_sem=send_sem.at[3],
                recv_sem=tp_sem.at[p],
                device_id={"tp": peer},
                device_id_type=MESH,
            ).start()
        tp_all[p, mt] = share
    for p in range(NP):
        fresh = tp_all.at[p, pl.ds(0, T - 1)]
        pltpu.make_async_copy(fresh, fresh, tp_sem.at[p]).wait()
        mixed = sum(tp_all[p, t].astype(jnp.float32) for t in range(T))
        for c in range(4):
            out_ref[:, COL4 * c + PC * p : COL4 * c + PC * (p + 1)] = mixed[
                4 * c : 4 * c + 4, :
            ].astype(jnp.bfloat16)

    for sem, part_ref in (
        (0, q_all.at[pl.ds(0, S - 1)]),
        (1, o_all.at[pl.ds(0, S - 1)]),
        (2, st_all.at[pl.ds(0, S - 1)]),
        (3, tp_all.at[:, pl.ds(0, T - 1)]),
    ):
        pltpu.make_async_copy(part_ref, part_ref, send_sem.at[sem]).wait()


def local(x, w, gain, q, rk, rv, pt, div, length, ow):
    bf16, f32, i32 = jnp.bfloat16, jnp.float32, jnp.int32
    hbm = pl.BlockSpec(memory_space=pl.ANY)
    V = pltpu.VMEM
    return pl.pallas_call(
        kernel,
        out_shape=jax.ShapeDtypeStruct((4, D), bf16),
        in_specs=[hbm] * 11,
        out_specs=pl.BlockSpec(memory_space=pltpu.VMEM),
        scratch_shapes=[
            V((ROWS, D), bf16),
            V((2 * D, HD), bf16),
            V((D, 256), bf16),
            V((1, HD), f32),
            V((4, 512), bf16),
            V((2048, HD), bf16),
            V((2048, HD), bf16),
            pltpu.SMEM((4, 4), i32),
            pltpu.SMEM((1, 128), i32),
            pltpu.SMEM((1, 128), i32),
            V((1, 128), i32),
            V((1, 128), i32),
            V((512, D), bf16),
            V((592, HD), f32),
            V((16, HD), bf16),
            V((16, HD), bf16),
            V((S, 16, HD), bf16),
            V((S, 16, HD), bf16),
            V((S, 16, HD), bf16),
            V((2 * GROUPS, 1, 128), f32),
            V((S, 1, 128), f32),
            V((128, 128), f32),
            V((NP, 16, PC), bf16),
            V((NP, T, 16, PC), bf16),
            pltpu.SemaphoreType.DMA((8,)),
            pltpu.SemaphoreType.DMA((2, NC)),
            pltpu.SemaphoreType.DMA((2,)),
            pltpu.SemaphoreType.DMA,
            pltpu.SemaphoreType.DMA((4,)),
            pltpu.SemaphoreType.DMA((2,)),
            pltpu.SemaphoreType.DMA((GROUPS,)),
            pltpu.SemaphoreType.DMA((NP,)),
        ],
        compiler_params=pltpu.CompilerParams(
            collective_id=0, has_side_effects=True, vmem_limit_bytes=40 * 1024 * 1024
        ),
        cost_estimate=pl.CostEstimate(
            flops=1_500_000_000, bytes_accessed=12_000_000, transcendentals=200_000
        ),
    )(
        *(
            pltpu.with_memory_space_constraint(operand, pltpu.HBM)
            for operand in (
                x,
                w.reshape(2 * D, HD),
                gain.reshape(1, HD),
                q,
                rk.reshape(2048, HD),
                rv.reshape(2048, HD),
                pt,
                div.reshape(1, 128),
                length.reshape(1, 128),
                ow,
                jnp.asarray(rope_table()),
            )
        )
    )


def solution(mesh):
    return jax.shard_map(
        local,
        mesh=mesh,
        in_specs=(
            P("samp", None),
            P(None, None, "tp"),
            P(),
            P("samp", "tp"),
            P("samp", None, "tp"),
            P("samp", None, "tp"),
            P("samp", None),
            P(),
            P(),
            P("tp", None),
        ),
        out_specs=P("samp", None),
        check_vma=False,
    )
```

```python
import numpy as np
import jax
import jax.numpy as jnp
from jax import lax
from jax.experimental import pallas as pl
from jax.experimental.pallas import tpu as pltpu
from jax.sharding import PartitionSpec as P

ROPE_BASE = 1000000.0
NORM_EPS = 1e-06
FLOOR = -1e30
S = 32
T = 8
HD = 128
D = 5120
ROWS = 256
NC = 5
DC = D // NC
COL4 = D // 4
PC = 640
NP = COL4 // PC
MESH = pl.DeviceIdType.MESH

COS0, SIN0, COSB, SINB, FREQ = 0, 256, 512, 544, 576
STEPX, STEPZ, PLACE = 577, 581, 585

STEPS = sorted(
    ((dx, dz) for dx in range(4) for dz in range(8)),
    key=lambda step: (min(step[0], 4 - step[0]) + min(step[1], 8 - step[1]), step),
)
BACK = [STEPS.index((-dx % 4, -dz % 8)) for dx, dz in STEPS]
GROUPS, PER = 4, 8


def rope_table():
    freq = ROPE_BASE ** (-(np.arange(64, dtype=np.float64) * 2.0 / HD))
    freq = np.concatenate([freq, freq])
    row = np.arange(ROWS, dtype=np.float64)[:, None] * freq
    base = (np.arange(S, dtype=np.float64) * ROWS)[:, None] * freq
    last = np.zeros((16, HD))
    last[0] = freq
    for slot in range(S):
        lanes = slice(slot % PER * 16, slot % PER * 16 + 16)
        last[STEPX - FREQ + slot // PER, lanes] = STEPS[slot][0]
        last[STEPZ - FREQ + slot // PER, lanes] = STEPS[slot][1]
        last[PLACE - FREQ, slot] = BACK[slot] % 4
    return np.concatenate([np.cos(row), np.sin(row), np.cos(base), np.sin(base), last]).astype(
        np.float32
    )


def samp_peer(me, slot):
    dx, dz = STEPS[slot]
    x = jnp.bitwise_and(lax.shift_right_logical(me, 3) + dx, 3)
    return x * 8 + jnp.bitwise_and(me + dz, 7)


def tp_peers(mt):
    for dy in (2, 1, 3, 0):
        same = lax.rem(mt + 2 * dy, T)
        if dy:
            yield same
        yield same + 1 - 2 * lax.rem(same, 2)


def swap_halves(v):
    lane = lax.broadcasted_iota(jnp.int32, v.shape, 1)
    return jnp.where(lane < 64, -1.0, 1.0) * pltpu.roll(v, 64, 1)


def kernel(
    x_hbm,
    w_hbm,
    gain_hbm,
    q_hbm,
    rk_hbm,
    rv_hbm,
    pt_hbm,
    div_hbm,
    len_hbm,
    ow_hbm,
    tab_hbm,
    out_ref,
    x_v,
    w_v,
    wd,
    gain_v,
    q_v,
    rk_v,
    rv_v,
    pt_s,
    div_s,
    len_s,
    div_v,
    len_v,
    ow_v,
    tab_v,
    q_send,
    q_res,
    q_all,
    o_send,
    o_all,
    st_send,
    st_all,
    tr_v,
    tp_send,
    tp_all,
    small_sem,
    chunk_sem,
    page_sem,
    ow_sem,
    send_sem,
    recv_sem,
    q_sem,
    tp_sem,
):
    me = lax.axis_index("samp")
    mt = lax.axis_index("tp")

    barrier = pltpu.get_barrier_semaphore()
    for slot in range(S - 1, 0, -1):
        pl.semaphore_signal(
            barrier, inc=1, device_id={"samp": samp_peer(me, slot)}, device_id_type=MESH
        )
    for peer in tp_peers(mt):
        pl.semaphore_signal(barrier, inc=1, device_id={"tp": peer}, device_id_type=MESH)

    small = [
        pltpu.make_async_copy(src, dst, small_sem.at[i])
        for i, (src, dst) in enumerate(
            [
                (len_hbm, len_s),
                (div_hbm, div_s),
                (q_hbm, q_v),
                (tab_hbm, tab_v),
                (pt_hbm, pt_s),
                (len_hbm, len_v),
                (div_hbm, div_v),
                (gain_hbm, gain_v),
            ]
        )
    ]
    for copy in small:
        copy.start()
    w_copies = [
        pltpu.make_async_copy(
            w_hbm.at[pl.ds(c * 2 * DC, 2 * DC)], w_v.at[pl.ds(c * 2 * DC, 2 * DC)], chunk_sem.at[0, c]
        )
        for c in range(NC)
    ]
    x_copies = [
        pltpu.make_async_copy(
            x_hbm.at[:, pl.ds(c * DC, DC)], x_v.at[:, pl.ds(c * DC, DC)], chunk_sem.at[1, c]
        )
        for c in range(NC)
    ]
    for copy in w_copies + x_copies:
        copy.start()
    pages = [
        pltpu.make_async_copy(rk_hbm, rk_v, page_sem.at[0]),
        pltpu.make_async_copy(rv_hbm, rv_v, page_sem.at[1]),
    ]
    for copy in pages:
        copy.start()
    ow_copy = pltpu.make_async_copy(ow_hbm, ow_v, ow_sem)
    ow_copy.start()

    for copy in small:
        copy.wait()
    row = lax.broadcasted_iota(jnp.int32, (16, HD), 0)
    sample = lax.rem(row, 4)

    def by_sample(values):
        return jnp.where(
            sample == 0,
            values[0],
            jnp.where(sample == 1, values[1], jnp.where(sample == 2, values[2], values[3])),
        )

    my_len = [len_s[0, me * 4 + i] for i in range(4)]
    my_div = [div_s[0, me * 4 + i] for i in range(4)]
    freq = tab_v[FREQ : FREQ + 1, :]
    q = q_v[...].astype(jnp.float32)
    q = jnp.concatenate([q[:, h * HD : (h + 1) * HD] for h in range(4)], axis=0)
    q_swapped = swap_halves(q)

    def rotate(positions):
        angle = by_sample(positions).astype(jnp.float32) * freq
        return (q * jnp.cos(angle) + q_swapped * jnp.sin(angle)).astype(jnp.bfloat16)

    q_app = rotate([my_len[i] - 128 * my_div[i] for i in range(4)])
    q_res[...] = rotate(my_len)
    q_send[...] = q_app
    q_all[0] = q_app

    pl.semaphore_wait(barrier, S - 1 + T - 1)

    for slot in range(S - 1, 0, -1):
        pltpu.make_async_remote_copy(
            src_ref=q_send,
            dst_ref=q_all.at[BACK[slot]],
            send_sem=send_sem.at[0],
            recv_sem=q_sem.at[BACK[slot] // PER],
            device_id={"samp": samp_peer(me, slot)},
            device_id_type=MESH,
        ).start()

    used = len_v[...] - 128 * div_v[...]
    high = lax.shift_right_logical(used, 7)
    low = used - 128 * high
    pair_row = lax.broadcasted_iota(jnp.int32, (16, 128), 0)
    pair = jnp.where(pair_row == 0, high, jnp.where(pair_row == 1, low, 0))
    pair = pair.astype(jnp.float32).astype(jnp.bfloat16)
    e_row = lax.broadcasted_iota(jnp.int32, (128, 128), 0)
    e_col = lax.broadcasted_iota(jnp.int32, (1, 128), 1)
    used_wide = []
    for g in range(GROUPS):
        step_x = tab_v[STEPX + g : STEPX + g + 1, :].astype(jnp.int32)
        step_z = tab_v[STEPZ + g : STEPZ + g + 1, :].astype(jnp.int32)
        owner = jnp.bitwise_and(step_x + lax.shift_right_logical(me, 3), 3) * 8
        owner = owner + jnp.bitwise_and(step_z + me, 7)
        spread = jnp.where(e_row == 4 * owner + jnp.bitwise_and(e_col, 3), 1.0, 0.0)
        wide = jnp.dot(pair, spread.astype(jnp.bfloat16), preferred_element_type=jnp.float32)
        used_wide.append((wide[0:1] * 128.0 + wide[1:2]).astype(jnp.int32))

    p_row = lax.broadcasted_iota(jnp.int32, (256, 256), 0)
    p_col = lax.broadcasted_iota(jnp.int32, (256, 256), 1)
    perm = jnp.where(
        p_col == jnp.where(p_row < 128, 2 * p_row, 2 * p_row - 255), 1.0, 0.0
    ).astype(jnp.bfloat16)
    for c in range(NC):
        w_copies[c].wait()
        for i in range(c * DC // 256, (c + 1) * DC // 256):
            pairs = jnp.concatenate(
                [w_v[pl.ds(i * 512, 256), :], w_v[pl.ds(i * 512 + 256, 256), :]], axis=1
            )
            apart = jnp.dot(perm, pairs, preferred_element_type=jnp.float32).astype(jnp.bfloat16)
            wd[pl.ds(i * 256, 128), 0:128] = apart[0:128, 0:128]
            wd[pl.ds(i * 256, 128), 128:256] = apart[128:256, 0:128]
            wd[pl.ds(i * 256 + 128, 128), 0:128] = apart[0:128, 128:256]
            wd[pl.ds(i * 256 + 128, 128), 128:256] = apart[128:256, 128:256]

    acc = jnp.zeros((ROWS, 256), jnp.float32)
    for c in range(NC):
        x_copies[c].wait()
        acc = acc + jnp.dot(
            x_v[:, c * DC : (c + 1) * DC],
            wd[c * DC : (c + 1) * DC, :],
            preferred_element_type=jnp.float32,
        )
    raw = acc[:, 0:128]
    values = acc[:, 128:256].astype(jnp.bfloat16)
    scale = lax.rsqrt(jnp.mean(raw * raw, axis=1, keepdims=True) + NORM_EPS)
    keys = raw * scale * gain_v[...]
    cos_b = tab_v[pl.ds(COSB + me, 1), :]
    sin_b = tab_v[pl.ds(SINB + me, 1), :]
    cos_0 = tab_v[COS0 : COS0 + ROWS, :]
    sin_0 = tab_v[SIN0 : SIN0 + ROWS, :]
    cos = cos_0 * cos_b - sin_0 * sin_b
    sin = sin_0 * cos_b + cos_0 * sin_b
    keys = (keys * cos + swap_halves(keys) * sin).astype(jnp.bfloat16)

    position = lax.broadcasted_iota(jnp.int32, (ROWS, PER * 16), 0) + me * ROWS
    for g in reversed(range(GROUPS)):
        first = 1 if g == 0 else PER * g
        fresh = q_all.at[pl.ds(first, PER * (g + 1) - first)]
        pltpu.make_async_copy(fresh, fresh, q_sem.at[g]).wait()
        scores = lax.dot_general(
            keys,
            q_all[PER * g : PER * (g + 1)].reshape(PER * 16, HD),
            (((1,), (1,)), ((), ())),
            preferred_element_type=jnp.float32,
        ) * (HD**-0.5)
        valid = position < used_wide[g]
        top = jnp.max(jnp.where(valid, scores, FLOOR), axis=0, keepdims=True)
        weights = jnp.where(valid, jnp.exp(scores - top), 0.0)
        total = jnp.sum(weights, axis=0, keepdims=True)
        for half in (0, 1):
            lanes = slice(64 * half, 64 * half + 64)
            st_send[2 * g + half] = jnp.concatenate([top[:, lanes], total[:, lanes]], axis=1)
        for slot in range(PER * (g + 1) - 1, first - 1, -1):
            pltpu.make_async_remote_copy(
                src_ref=st_send.at[slot // 4],
                dst_ref=st_all.at[BACK[slot]],
                send_sem=send_sem.at[2],
                recv_sem=recv_sem.at[1],
                device_id={"samp": samp_peer(me, slot)},
                device_id_type=MESH,
            ).start()
        part = lax.dot_general(
            weights.astype(jnp.bfloat16),
            values,
            (((0,), (0,)), ((), ())),
            preferred_element_type=jnp.float32,
        ).astype(jnp.bfloat16)
        o_send[PER * g : PER * (g + 1)] = part.reshape(PER, 16, HD)
        for slot in range(PER * (g + 1) - 1, first - 1, -1):
            pltpu.make_async_remote_copy(
                src_ref=o_send.at[slot],
                dst_ref=o_all.at[BACK[slot]],
                send_sem=send_sem.at[1],
                recv_sem=recv_sem.at[0],
                device_id={"samp": samp_peer(me, slot)},
                device_id_type=MESH,
            ).start()
    o_all[0] = o_send[0]
    st_all[0] = st_send[0]

    for copy in pages:
        copy.wait()
    lane = lax.broadcasted_iota(jnp.int32, (16, HD), 1)
    slot_ok = jnp.zeros((16, HD), jnp.float32)
    for j in range(4):
        page = by_sample([pt_s[i, j] for i in range(4)])
        count = by_sample(my_div)
        slot_ok = jnp.where((lane == page) & (count > j), 1.0, slot_ok)
    seen = jnp.concatenate(
        [jnp.broadcast_to(slot_ok[:, k : k + 1], (16, HD)) for k in range(16)], axis=1
    ) > 0.5
    res_scores = lax.dot_general(
        q_res[...], rk_v[...], (((1,), (1,)), ((), ())), preferred_element_type=jnp.float32
    ) * (HD**-0.5)
    res_top = jnp.max(jnp.where(seen, res_scores, FLOOR), axis=1, keepdims=True)
    res_weights = jnp.where(seen, jnp.exp(res_scores - res_top), 0.0)
    res_total = jnp.sum(res_weights, axis=1, keepdims=True)
    res_part = jnp.dot(
        res_weights.astype(jnp.bfloat16), rv_v[...], preferred_element_type=jnp.float32
    )

    pltpu.make_async_copy(
        st_all.at[pl.ds(0, S - 1)], st_all.at[pl.ds(0, S - 1)], recv_sem.at[1]
    ).wait()
    tr_v[...] = jnp.concatenate(
        [st_all[:, 0, :], jnp.zeros((128 - S, 128), jnp.float32)], axis=0
    ).T
    place = jnp.broadcast_to(tab_v[PLACE : PLACE + 1, :], (16, HD))
    tops, totals = tr_v[0:16, :], tr_v[64:80, :]
    for n in range(1, 4):
        tops = jnp.where(place == float(n), tr_v[16 * n : 16 * n + 16, :], tops)
        totals = jnp.where(place == float(n), tr_v[16 * n + 64 : 16 * n + 80, :], totals)
    tops = jnp.where(lane < S, tops, FLOOR)
    highest = jnp.maximum(jnp.max(tops, axis=1, keepdims=True), res_top)
    factor = jnp.exp(tops - highest)
    res_factor = jnp.exp(res_top - highest)
    whole = jnp.sum(factor * totals, axis=1, keepdims=True) + res_factor * res_total
    pltpu.make_async_copy(
        o_all.at[pl.ds(0, S - 1)], o_all.at[pl.ds(0, S - 1)], recv_sem.at[0]
    ).wait()
    attended = [res_part * res_factor] + [jnp.zeros((16, HD), jnp.float32)] * 3
    for i in range(S):
        attended[i % 4] = attended[i % 4] + factor[:, i : i + 1] * o_all[i].astype(jnp.float32)
    attended = (attended[0] + attended[1] + attended[2] + attended[3]) / whole
    turned = [attended] + [pltpu.roll(attended, 4 * n, 0) for n in range(1, 4)]

    ow_copy.wait()
    group = lax.shift_right_logical(lax.broadcasted_iota(jnp.int32, (16, 512), 0), 2)
    placed = [
        jnp.where(
            group == c, jnp.concatenate([turned[(c - h) % 4] for h in range(4)], axis=1), 0.0
        ).astype(jnp.bfloat16)
        for c in range(4)
    ]
    for p in range(NP):
        share = sum(
            jnp.dot(
                placed[c],
                ow_v[:, COL4 * c + PC * p : COL4 * c + PC * (p + 1)],
                preferred_element_type=jnp.float32,
            )
            for c in range(4)
        ).astype(jnp.bfloat16)
        tp_send[p] = share
        for peer in tp_peers(mt):
            pltpu.make_async_remote_copy(
                src_ref=tp_send.at[p],
                dst_ref=tp_all.at[p, mt],
                send_sem=send_sem.at[3],
                recv_sem=tp_sem.at[p],
                device_id={"tp": peer},
                device_id_type=MESH,
            ).start()
        tp_all[p, mt] = share
    for p in range(NP):
        fresh = tp_all.at[p, pl.ds(0, T - 1)]
        pltpu.make_async_copy(fresh, fresh, tp_sem.at[p]).wait()
        mixed = sum(tp_all[p, t].astype(jnp.float32) for t in range(T))
        for c in range(4):
            out_ref[:, COL4 * c + PC * p : COL4 * c + PC * (p + 1)] = mixed[
                4 * c : 4 * c + 4, :
            ].astype(jnp.bfloat16)

    for sem, part_ref in (
        (0, q_all.at[pl.ds(0, S - 1)]),
        (1, o_all.at[pl.ds(0, S - 1)]),
        (2, st_all.at[pl.ds(0, S - 1)]),
        (3, tp_all.at[:, pl.ds(0, T - 1)]),
    ):
        pltpu.make_async_copy(part_ref, part_ref, send_sem.at[sem]).wait()


def local(x, w, gain, q, rk, rv, pt, div, length, ow):
    bf16, f32, i32 = jnp.bfloat16, jnp.float32, jnp.int32
    hbm = pl.BlockSpec(memory_space=pl.ANY)
    V = pltpu.VMEM
    return pl.pallas_call(
        kernel,
        out_shape=jax.ShapeDtypeStruct((4, D), bf16),
        in_specs=[hbm] * 11,
        out_specs=pl.BlockSpec(memory_space=pltpu.VMEM),
        scratch_shapes=[
            V((ROWS, D), bf16),
            V((2 * D, HD), bf16),
            V((D, 256), bf16),
            V((1, HD), f32),
            V((4, 512), bf16),
            V((2048, HD), bf16),
            V((2048, HD), bf16),
            pltpu.SMEM((4, 4), i32),
            pltpu.SMEM((1, 128), i32),
            pltpu.SMEM((1, 128), i32),
            V((1, 128), i32),
            V((1, 128), i32),
            V((512, D), bf16),
            V((592, HD), f32),
            V((16, HD), bf16),
            V((16, HD), bf16),
            V((S, 16, HD), bf16),
            V((S, 16, HD), bf16),
            V((S, 16, HD), bf16),
            V((2 * GROUPS, 1, 128), f32),
            V((S, 1, 128), f32),
            V((128, 128), f32),
            V((NP, 16, PC), bf16),
            V((NP, T, 16, PC), bf16),
            pltpu.SemaphoreType.DMA((8,)),
            pltpu.SemaphoreType.DMA((2, NC)),
            pltpu.SemaphoreType.DMA((2,)),
            pltpu.SemaphoreType.DMA,
            pltpu.SemaphoreType.DMA((4,)),
            pltpu.SemaphoreType.DMA((2,)),
            pltpu.SemaphoreType.DMA((GROUPS,)),
            pltpu.SemaphoreType.DMA((NP,)),
        ],
        compiler_params=pltpu.CompilerParams(
            collective_id=0, has_side_effects=True, vmem_limit_bytes=40 * 1024 * 1024
        ),
        cost_estimate=pl.CostEstimate(
            flops=1_500_000_000, bytes_accessed=12_000_000, transcendentals=200_000
        ),
    )(
        *(
            pltpu.with_memory_space_constraint(operand, pltpu.HBM)
            for operand in (
                x,
                w.reshape(2 * D, HD),
                gain.reshape(1, HD),
                q,
                rk.reshape(2048, HD),
                rv.reshape(2048, HD),
                pt,
                div.reshape(1, 128),
                length.reshape(1, 128),
                ow,
                jnp.asarray(rope_table()),
            )
        )
    )


def solution(mesh):
    return jax.shard_map(
        local,
        mesh=mesh,
        in_specs=(
            P("samp", None),
            P(None, None, "tp"),
            P(),
            P("samp", "tp"),
            P("samp", None, "tp"),
            P("samp", None, "tp"),
            P("samp", None),
            P(),
            P(),
            P("tp", None),
        ),
        out_specs=P("samp", None),
        check_vma=False,
    )
```

```python
import numpy as np
import jax
import jax.numpy as jnp
from jax import lax
from jax.experimental import pallas as pl
from jax.experimental.pallas import tpu as pltpu
from jax.sharding import PartitionSpec as P

ROPE_BASE = 1000000.0
NORM_EPS = 1e-06
FLOOR = -1e30
S = 32
T = 8
HD = 128
D = 5120
ROWS = 256
NC = 5
DC = D // NC
COL4 = D // 4
PC = 640
NP = COL4 // PC
MESH = pl.DeviceIdType.MESH

COS0, SIN0, COSB, SINB, FREQ = 0, 256, 512, 544, 576
STEPX, STEPZ, PLACE = 577, 581, 585

STEPS = sorted(
    ((dx, dz) for dx in range(4) for dz in range(8)),
    key=lambda step: (min(step[0], 4 - step[0]) + 2 * min(step[1], 8 - step[1]), step),
)
BACK = [STEPS.index((-dx % 4, -dz % 8)) for dx, dz in STEPS]
GROUPS, PER = 4, 8


def rope_table():
    freq = ROPE_BASE ** (-(np.arange(64, dtype=np.float64) * 2.0 / HD))
    freq = np.concatenate([freq, freq])
    row = np.arange(ROWS, dtype=np.float64)[:, None] * freq
    base = (np.arange(S, dtype=np.float64) * ROWS)[:, None] * freq
    last = np.zeros((16, HD))
    last[0] = freq
    for slot in range(S):
        lanes = slice(slot % PER * 16, slot % PER * 16 + 16)
        last[STEPX - FREQ + slot // PER, lanes] = STEPS[slot][0]
        last[STEPZ - FREQ + slot // PER, lanes] = STEPS[slot][1]
        last[PLACE - FREQ, slot] = BACK[slot] % 4
    return np.concatenate([np.cos(row), np.sin(row), np.cos(base), np.sin(base), last]).astype(
        np.float32
    )


def samp_peer(me, slot):
    dx, dz = STEPS[slot]
    x = jnp.bitwise_and(lax.shift_right_logical(me, 3) + dx, 3)
    return x * 8 + jnp.bitwise_and(me + dz, 7)


def tp_peers(mt):
    for dy in (2, 1, 3, 0):
        same = lax.rem(mt + 2 * dy, T)
        if dy:
            yield same
        yield same + 1 - 2 * lax.rem(same, 2)


def swap_halves(v):
    lane = lax.broadcasted_iota(jnp.int32, v.shape, 1)
    return jnp.where(lane < 64, -1.0, 1.0) * pltpu.roll(v, 64, 1)


def kernel(
    x_hbm,
    w_hbm,
    gain_hbm,
    q_hbm,
    rk_hbm,
    rv_hbm,
    pt_hbm,
    div_hbm,
    len_hbm,
    ow_hbm,
    tab_hbm,
    out_ref,
    x_v,
    w_v,
    wd,
    gain_v,
    q_v,
    rk_v,
    rv_v,
    pt_s,
    div_s,
    len_s,
    div_v,
    len_v,
    ow_v,
    tab_v,
    q_send,
    q_res,
    q_all,
    o_send,
    o_all,
    st_send,
    st_all,
    tr_v,
    tp_send,
    tp_all,
    small_sem,
    chunk_sem,
    page_sem,
    ow_sem,
    send_sem,
    recv_sem,
    q_sem,
    tp_sem,
):
    me = lax.axis_index("samp")
    mt = lax.axis_index("tp")

    barrier = pltpu.get_barrier_semaphore()
    for slot in range(S - 1, 0, -1):
        pl.semaphore_signal(
            barrier, inc=1, device_id={"samp": samp_peer(me, slot)}, device_id_type=MESH
        )
    for peer in tp_peers(mt):
        pl.semaphore_signal(barrier, inc=1, device_id={"tp": peer}, device_id_type=MESH)

    small = [
        pltpu.make_async_copy(src, dst, small_sem.at[i])
        for i, (src, dst) in enumerate(
            [
                (len_hbm, len_s),
                (div_hbm, div_s),
                (q_hbm, q_v),
                (tab_hbm, tab_v),
                (pt_hbm, pt_s),
                (len_hbm, len_v),
                (div_hbm, div_v),
                (gain_hbm, gain_v),
            ]
        )
    ]
    for copy in small:
        copy.start()
    w_copies = [
        pltpu.make_async_copy(
            w_hbm.at[pl.ds(c * 2 * DC, 2 * DC)], w_v.at[pl.ds(c * 2 * DC, 2 * DC)], chunk_sem.at[0, c]
        )
        for c in range(NC)
    ]
    x_copies = [
        pltpu.make_async_copy(
            x_hbm.at[:, pl.ds(c * DC, DC)], x_v.at[:, pl.ds(c * DC, DC)], chunk_sem.at[1, c]
        )
        for c in range(NC)
    ]
    for copy in w_copies + x_copies:
        copy.start()
    pages = [
        pltpu.make_async_copy(rk_hbm, rk_v, page_sem.at[0]),
        pltpu.make_async_copy(rv_hbm, rv_v, page_sem.at[1]),
    ]
    for copy in pages:
        copy.start()
    ow_copy = pltpu.make_async_copy(ow_hbm, ow_v, ow_sem)
    ow_copy.start()

    for copy in small:
        copy.wait()
    row = lax.broadcasted_iota(jnp.int32, (16, HD), 0)
    sample = lax.rem(row, 4)

    def by_sample(values):
        return jnp.where(
            sample == 0,
            values[0],
            jnp.where(sample == 1, values[1], jnp.where(sample == 2, values[2], values[3])),
        )

    my_len = [len_s[0, me * 4 + i] for i in range(4)]
    my_div = [div_s[0, me * 4 + i] for i in range(4)]
    freq = tab_v[FREQ : FREQ + 1, :]
    q = q_v[...].astype(jnp.float32)
    q = jnp.concatenate([q[:, h * HD : (h + 1) * HD] for h in range(4)], axis=0)
    q_swapped = swap_halves(q)

    def rotate(positions):
        angle = by_sample(positions).astype(jnp.float32) * freq
        return (q * jnp.cos(angle) + q_swapped * jnp.sin(angle)).astype(jnp.bfloat16)

    q_app = rotate([my_len[i] - 128 * my_div[i] for i in range(4)])
    q_res[...] = rotate(my_len)
    q_send[...] = q_app
    q_all[0] = q_app

    pl.semaphore_wait(barrier, S - 1 + T - 1)

    for slot in range(S - 1, 0, -1):
        pltpu.make_async_remote_copy(
            src_ref=q_send,
            dst_ref=q_all.at[BACK[slot]],
            send_sem=send_sem.at[0],
            recv_sem=q_sem.at[BACK[slot] // PER],
            device_id={"samp": samp_peer(me, slot)},
            device_id_type=MESH,
        ).start()

    used = len_v[...] - 128 * div_v[...]
    high = lax.shift_right_logical(used, 7)
    low = used - 128 * high
    pair_row = lax.broadcasted_iota(jnp.int32, (16, 128), 0)
    pair = jnp.where(pair_row == 0, high, jnp.where(pair_row == 1, low, 0))
    pair = pair.astype(jnp.float32).astype(jnp.bfloat16)
    e_row = lax.broadcasted_iota(jnp.int32, (128, 128), 0)
    e_col = lax.broadcasted_iota(jnp.int32, (1, 128), 1)
    used_wide = []
    for g in range(GROUPS):
        step_x = tab_v[STEPX + g : STEPX + g + 1, :].astype(jnp.int32)
        step_z = tab_v[STEPZ + g : STEPZ + g + 1, :].astype(jnp.int32)
        owner = jnp.bitwise_and(step_x + lax.shift_right_logical(me, 3), 3) * 8
        owner = owner + jnp.bitwise_and(step_z + me, 7)
        spread = jnp.where(e_row == 4 * owner + jnp.bitwise_and(e_col, 3), 1.0, 0.0)
        wide = jnp.dot(pair, spread.astype(jnp.bfloat16), preferred_element_type=jnp.float32)
        used_wide.append((wide[0:1] * 128.0 + wide[1:2]).astype(jnp.int32))

    p_row = lax.broadcasted_iota(jnp.int32, (256, 256), 0)
    p_col = lax.broadcasted_iota(jnp.int32, (256, 256), 1)
    perm = jnp.where(
        p_col == jnp.where(p_row < 128, 2 * p_row, 2 * p_row - 255), 1.0, 0.0
    ).astype(jnp.bfloat16)
    for c in range(NC):
        w_copies[c].wait()
        for i in range(c * DC // 256, (c + 1) * DC // 256):
            pairs = jnp.concatenate(
                [w_v[pl.ds(i * 512, 256), :], w_v[pl.ds(i * 512 + 256, 256), :]], axis=1
            )
            apart = jnp.dot(perm, pairs, preferred_element_type=jnp.float32).astype(jnp.bfloat16)
            wd[pl.ds(i * 256, 128), 0:128] = apart[0:128, 0:128]
            wd[pl.ds(i * 256, 128), 128:256] = apart[128:256, 0:128]
            wd[pl.ds(i * 256 + 128, 128), 0:128] = apart[0:128, 128:256]
            wd[pl.ds(i * 256 + 128, 128), 128:256] = apart[128:256, 128:256]

    acc = jnp.zeros((ROWS, 256), jnp.float32)
    for c in range(NC):
        x_copies[c].wait()
        acc = acc + jnp.dot(
            x_v[:, c * DC : (c + 1) * DC],
            wd[c * DC : (c + 1) * DC, :],
            preferred_element_type=jnp.float32,
        )
    raw = acc[:, 0:128]
    values = acc[:, 128:256].astype(jnp.bfloat16)
    scale = lax.rsqrt(jnp.mean(raw * raw, axis=1, keepdims=True) + NORM_EPS)
    keys = raw * scale * gain_v[...]
    cos_b = tab_v[pl.ds(COSB + me, 1), :]
    sin_b = tab_v[pl.ds(SINB + me, 1), :]
    cos_0 = tab_v[COS0 : COS0 + ROWS, :]
    sin_0 = tab_v[SIN0 : SIN0 + ROWS, :]
    cos = cos_0 * cos_b - sin_0 * sin_b
    sin = sin_0 * cos_b + cos_0 * sin_b
    keys = (keys * cos + swap_halves(keys) * sin).astype(jnp.bfloat16)

    position = lax.broadcasted_iota(jnp.int32, (ROWS, PER * 16), 0) + me * ROWS
    for g in reversed(range(GROUPS)):
        first = 1 if g == 0 else PER * g
        fresh = q_all.at[pl.ds(first, PER * (g + 1) - first)]
        pltpu.make_async_copy(fresh, fresh, q_sem.at[g]).wait()
        scores = lax.dot_general(
            keys,
            q_all[PER * g : PER * (g + 1)].reshape(PER * 16, HD),
            (((1,), (1,)), ((), ())),
            preferred_element_type=jnp.float32,
        ) * (HD**-0.5)
        valid = position < used_wide[g]
        top = jnp.max(jnp.where(valid, scores, FLOOR), axis=0, keepdims=True)
        weights = jnp.where(valid, jnp.exp(scores - top), 0.0)
        total = jnp.sum(weights, axis=0, keepdims=True)
        part = lax.dot_general(
            weights.astype(jnp.bfloat16),
            values,
            (((0,), (0,)), ((), ())),
            preferred_element_type=jnp.float32,
        ).astype(jnp.bfloat16)
        o_send[PER * g : PER * (g + 1)] = part.reshape(PER, 16, HD)
        for half in (0, 1):
            lanes = slice(64 * half, 64 * half + 64)
            st_send[2 * g + half] = jnp.concatenate([top[:, lanes], total[:, lanes]], axis=1)
        for slot in range(PER * (g + 1) - 1, first - 1, -1):
            pltpu.make_async_remote_copy(
                src_ref=st_send.at[slot // 4],
                dst_ref=st_all.at[BACK[slot]],
                send_sem=send_sem.at[2],
                recv_sem=recv_sem.at[1],
                device_id={"samp": samp_peer(me, slot)},
                device_id_type=MESH,
            ).start()
            pltpu.make_async_remote_copy(
                src_ref=o_send.at[slot],
                dst_ref=o_all.at[BACK[slot]],
                send_sem=send_sem.at[1],
                recv_sem=recv_sem.at[0],
                device_id={"samp": samp_peer(me, slot)},
                device_id_type=MESH,
            ).start()
    o_all[0] = o_send[0]
    st_all[0] = st_send[0]

    for copy in pages:
        copy.wait()
    lane = lax.broadcasted_iota(jnp.int32, (16, HD), 1)
    slot_ok = jnp.zeros((16, HD), jnp.float32)
    for j in range(4):
        page = by_sample([pt_s[i, j] for i in range(4)])
        count = by_sample(my_div)
        slot_ok = jnp.where((lane == page) & (count > j), 1.0, slot_ok)
    seen = jnp.concatenate(
        [jnp.broadcast_to(slot_ok[:, k : k + 1], (16, HD)) for k in range(16)], axis=1
    ) > 0.5
    res_scores = lax.dot_general(
        q_res[...], rk_v[...], (((1,), (1,)), ((), ())), preferred_element_type=jnp.float32
    ) * (HD**-0.5)
    res_top = jnp.max(jnp.where(seen, res_scores, FLOOR), axis=1, keepdims=True)
    res_weights = jnp.where(seen, jnp.exp(res_scores - res_top), 0.0)
    res_total = jnp.sum(res_weights, axis=1, keepdims=True)
    res_part = jnp.dot(
        res_weights.astype(jnp.bfloat16), rv_v[...], preferred_element_type=jnp.float32
    )

    pltpu.make_async_copy(
        st_all.at[pl.ds(0, S - 1)], st_all.at[pl.ds(0, S - 1)], recv_sem.at[1]
    ).wait()
    tr_v[...] = jnp.concatenate(
        [st_all[:, 0, :], jnp.zeros((128 - S, 128), jnp.float32)], axis=0
    ).T
    place = jnp.broadcast_to(tab_v[PLACE : PLACE + 1, :], (16, HD))
    tops, totals = tr_v[0:16, :], tr_v[64:80, :]
    for n in range(1, 4):
        tops = jnp.where(place == float(n), tr_v[16 * n : 16 * n + 16, :], tops)
        totals = jnp.where(place == float(n), tr_v[16 * n + 64 : 16 * n + 80, :], totals)
    tops = jnp.where(lane < S, tops, FLOOR)
    highest = jnp.maximum(jnp.max(tops, axis=1, keepdims=True), res_top)
    factor = jnp.exp(tops - highest)
    res_factor = jnp.exp(res_top - highest)
    whole = jnp.sum(factor * totals, axis=1, keepdims=True) + res_factor * res_total
    pltpu.make_async_copy(
        o_all.at[pl.ds(0, S - 1)], o_all.at[pl.ds(0, S - 1)], recv_sem.at[0]
    ).wait()
    attended = [res_part * res_factor] + [jnp.zeros((16, HD), jnp.float32)] * 3
    for i in range(S):
        attended[i % 4] = attended[i % 4] + factor[:, i : i + 1] * o_all[i].astype(jnp.float32)
    attended = (attended[0] + attended[1] + attended[2] + attended[3]) / whole
    turned = [attended] + [pltpu.roll(attended, 4 * n, 0) for n in range(1, 4)]

    ow_copy.wait()
    group = lax.shift_right_logical(lax.broadcasted_iota(jnp.int32, (16, 512), 0), 2)
    placed = [
        jnp.where(
            group == c, jnp.concatenate([turned[(c - h) % 4] for h in range(4)], axis=1), 0.0
        ).astype(jnp.bfloat16)
        for c in range(4)
    ]
    for p in range(NP):
        share = sum(
            jnp.dot(
                placed[c],
                ow_v[:, COL4 * c + PC * p : COL4 * c + PC * (p + 1)],
                preferred_element_type=jnp.float32,
            )
            for c in range(4)
        ).astype(jnp.bfloat16)
        tp_send[p] = share
        for peer in tp_peers(mt):
            pltpu.make_async_remote_copy(
                src_ref=tp_send.at[p],
                dst_ref=tp_all.at[p, mt],
                send_sem=send_sem.at[3],
                recv_sem=tp_sem.at[p],
                device_id={"tp": peer},
                device_id_type=MESH,
            ).start()
        tp_all[p, mt] = share
    for p in range(NP):
        fresh = tp_all.at[p, pl.ds(0, T - 1)]
        pltpu.make_async_copy(fresh, fresh, tp_sem.at[p]).wait()
        mixed = sum(tp_all[p, t].astype(jnp.float32) for t in range(T))
        for c in range(4):
            out_ref[:, COL4 * c + PC * p : COL4 * c + PC * (p + 1)] = mixed[
                4 * c : 4 * c + 4, :
            ].astype(jnp.bfloat16)

    for sem, part_ref in (
        (0, q_all.at[pl.ds(0, S - 1)]),
        (1, o_all.at[pl.ds(0, S - 1)]),
        (2, st_all.at[pl.ds(0, S - 1)]),
        (3, tp_all.at[:, pl.ds(0, T - 1)]),
    ):
        pltpu.make_async_copy(part_ref, part_ref, send_sem.at[sem]).wait()


def local(x, w, gain, q, rk, rv, pt, div, length, ow):
    bf16, f32, i32 = jnp.bfloat16, jnp.float32, jnp.int32
    hbm = pl.BlockSpec(memory_space=pl.ANY)
    V = pltpu.VMEM
    return pl.pallas_call(
        kernel,
        out_shape=jax.ShapeDtypeStruct((4, D), bf16),
        in_specs=[hbm] * 11,
        out_specs=pl.BlockSpec(memory_space=pltpu.VMEM),
        scratch_shapes=[
            V((ROWS, D), bf16),
            V((2 * D, HD), bf16),
            V((D, 256), bf16),
            V((1, HD), f32),
            V((4, 512), bf16),
            V((2048, HD), bf16),
            V((2048, HD), bf16),
            pltpu.SMEM((4, 4), i32),
            pltpu.SMEM((1, 128), i32),
            pltpu.SMEM((1, 128), i32),
            V((1, 128), i32),
            V((1, 128), i32),
            V((512, D), bf16),
            V((592, HD), f32),
            V((16, HD), bf16),
            V((16, HD), bf16),
            V((S, 16, HD), bf16),
            V((S, 16, HD), bf16),
            V((S, 16, HD), bf16),
            V((2 * GROUPS, 1, 128), f32),
            V((S, 1, 128), f32),
            V((128, 128), f32),
            V((NP, 16, PC), bf16),
            V((NP, T, 16, PC), bf16),
            pltpu.SemaphoreType.DMA((8,)),
            pltpu.SemaphoreType.DMA((2, NC)),
            pltpu.SemaphoreType.DMA((2,)),
            pltpu.SemaphoreType.DMA,
            pltpu.SemaphoreType.DMA((4,)),
            pltpu.SemaphoreType.DMA((2,)),
            pltpu.SemaphoreType.DMA((GROUPS,)),
            pltpu.SemaphoreType.DMA((NP,)),
        ],
        compiler_params=pltpu.CompilerParams(
            collective_id=0, has_side_effects=True, vmem_limit_bytes=40 * 1024 * 1024
        ),
        cost_estimate=pl.CostEstimate(
            flops=1_500_000_000, bytes_accessed=12_000_000, transcendentals=200_000
        ),
    )(
        *(
            pltpu.with_memory_space_constraint(operand, pltpu.HBM)
            for operand in (
                x,
                w.reshape(2 * D, HD),
                gain.reshape(1, HD),
                q,
                rk.reshape(2048, HD),
                rv.reshape(2048, HD),
                pt,
                div.reshape(1, 128),
                length.reshape(1, 128),
                ow,
                jnp.asarray(rope_table()),
            )
        )
    )


def solution(mesh):
    return jax.shard_map(
        local,
        mesh=mesh,
        in_specs=(
            P("samp", None),
            P(None, None, "tp"),
            P(),
            P("samp", "tp"),
            P("samp", None, "tp"),
            P("samp", None, "tp"),
            P("samp", None),
            P(),
            P(),
            P("tp", None),
        ),
        out_specs=P("samp", None),
        check_vma=False,
    )
```
